512 devices in a mesh: row: 32 (over y, x), col: 16 (over z, core).
Axes of the slice: x: 4, y: 8, z: 8, core: 2. Of those that a mesh axis runs over, the one named last changes fastest.
Arguments:
- homolog_representation: bfloat16 [256, 512, 64], P('row', 'col'), may hold values from -1.5 to 1.5
- pair_state: bfloat16 [512, 512, 128], P('row', 'col'), may hold values from -6 to 6
- homolog_present: int32 [256], replicated, may hold values 0 or 1
- token_live_mask: int32 [512], replicated, may hold values 0 or 1
- product_projection: bfloat16 [64, 64], replicated, may hold values from -0.75 to 0.75
- mean_matrix: bfloat16 [1024, 128], replicated, may hold values from -0.75 to 0.75
- score_matrix: float32 [128, 8], replicated, may hold values from -17.5 to 17.5
- payload_projection: bfloat16 [64, 256], replicated, may hold values from -0.75 to 0.75
- switch_projection: bfloat16 [64, 256], replicated, may hold values from -0.75 to 0.75
- return_projection: bfloat16 [256, 64], replicated, may hold values from -1.5 to 1.5
- transition_input: bfloat16 [128, 1024], replicated, may hold values from -0.5 to 0.5
- transition_output: bfloat16 [512, 128], replicated, may hold values from -0.25 to 0.25
Outputs:
- alignment_output: bfloat16 [256, 512, 64], P('row', 'col')
- pair_output: bfloat16 [512, 512, 128], P('row', 'col')
The draws below stay inside these ranges and needn't reach their ends.
All inputs are finite; a program needn't handle non-finite values.
Results may differ from the reference program's by a relative error of at most 0.038.
Values may be sent and summed in bfloat16 or wider, within the bound.
A program may use at most 64 MiB of HBM per device.

```python
import jax
import jax.numpy as jnp
from jax import lax

HOMOLOG_FEATURES = 64
CZ = 128
PRODUCT_FEATURES = 32
BLEND_GROUPS = 8
GROUP_FEATURES = 32
FF = 512
TOK_ROW = 16
RESIDUE_SPAN = 512
HOMOLOG_DEPTH = 256


def spread_scales(key, low, high):
    raw = jax.random.uniform(key, (BLEND_GROUPS,), jnp.float32, 0.0, 1.0)
    placed = (raw - jnp.min(raw)) / (jnp.max(raw) - jnp.min(raw) + 1e-06)
    return jnp.exp(jnp.log(low) + placed * (jnp.log(high) - jnp.log(low)))


def draw_score_matrix(key, part):
    first_key = jax.random.fold_in(jax.random.fold_in(key, 17), 0)
    third_key = jax.random.fold_in(jax.random.fold_in(key, 17), 2)
    head_scale = spread_scales(first_key, 0.008, 0.25)
    base_draw = jnp.clip(jax.random.normal(third_key, (CZ, BLEND_GROUPS), jnp.float32), -4.8, 4.8)
    return base_draw * head_scale[None, :]


def plant(entries, rng, smallest, top_value):
    dims = entries.shape
    spot = [jax.random.randint(jax.random.fold_in(rng, axis), (), 0, dims[axis]) for axis in range(len(dims))]
    entries = entries.at[tuple(spot)].set(smallest)
    longest = dims.index(max(dims))
    spot[longest] = (spot[longest] + 1) % dims[longest]
    return entries.at[tuple(spot)].set(top_value)


def steps_of(own_key, dims, pieces, least, largest):
    factor_of, own = 1.0, jax.random.fold_in(own_key, 6)
    for dim, shards_of in pieces:
        heights = jnp.exp(jax.random.uniform(jax.random.fold_in(own, dim), (shards_of,), jnp.float32, least / len(pieces), largest / len(pieces)))
        factor_of = factor_of * jnp.repeat(heights, dims[dim] // shards_of).reshape([-1 if axis == dim else 1 for axis in range(len(dims))])
    return factor_of


def noise(own_key, shape, scale, limit, shards=(), kind=jnp.bfloat16):
    factor_of = steps_of(own_key, shape, shards, -0.22, 0.18) if shards else 1.0
    entries = jax.random.normal(own_key, shape, jnp.float32) * scale * factor_of
    return jnp.minimum(jnp.maximum(entries, -limit), limit).astype(kind)


def setup_inputs(seed: int = 0) -> dict:
    key_of = jax.random.split(jax.random.key(seed), 13)
    return {
        "homolog_representation": noise(key_of[0], (HOMOLOG_DEPTH, RESIDUE_SPAN, HOMOLOG_FEATURES), 0.1, 1.5, ((0, 32), (1, 16))),
        "pair_state": noise(key_of[1], (RESIDUE_SPAN, RESIDUE_SPAN, CZ), 1.0, 6.0, ((0, 32), (1, 16))),
        "homolog_present": plant((jax.random.randint(key_of[2], (HOMOLOG_DEPTH,), 0, 4) < 3).astype(jnp.int32), jax.random.fold_in(key_of[2], 1), 0, 1),
        "token_live_mask": plant((jax.random.randint(key_of[3], (RESIDUE_SPAN,), 0, 8) < 7).astype(jnp.int32), jax.random.fold_in(key_of[3], 1), 0, 1),
        "product_projection": noise(key_of[4], (HOMOLOG_FEATURES, 2 * PRODUCT_FEATURES), HOMOLOG_FEATURES ** -0.5, 0.75),
        "mean_matrix": noise(key_of[5], (PRODUCT_FEATURES * PRODUCT_FEATURES, CZ), 64 ** -0.5, 0.75),
        "score_matrix": draw_score_matrix(jax.random.fold_in(key_of[12], 71), 0),
        "payload_projection": noise(key_of[7], (HOMOLOG_FEATURES, BLEND_GROUPS * GROUP_FEATURES), HOMOLOG_FEATURES ** -0.5, 0.75),
        "switch_projection": noise(key_of[8], (HOMOLOG_FEATURES, BLEND_GROUPS * GROUP_FEATURES), HOMOLOG_FEATURES ** -0.5, 0.75),
        "return_projection": noise(key_of[9], (BLEND_GROUPS * GROUP_FEATURES, HOMOLOG_FEATURES), 16 ** -0.5, 1.5),
        "transition_input": noise(key_of[10], (CZ, 2 * FF), CZ ** -0.5, 0.5),
        "transition_output": noise(key_of[11], (FF, CZ), FF ** -0.5, 0.25),
    }


epsilon = 1e-05

def normalized_rows(source):
    source = source.astype(jnp.float32)
    center = source - lax.optimization_barrier(jnp.mean(source, axis=-1, keepdims=True))
    spread = lax.optimization_barrier(jnp.mean(center * center, axis=-1, keepdims=True))
    return center * lax.rsqrt(spread + epsilon)

def reference(homolog_representation, pair_state, homolog_present, token_live_mask, product_projection, mean_matrix, score_matrix, payload_projection, switch_projection, return_projection, transition_input, transition_output):
    homolog_standardized = normalized_rows(homolog_representation).astype(jnp.bfloat16)
    homolog_reshaped = homolog_standardized.reshape(HOMOLOG_DEPTH * RESIDUE_SPAN, HOMOLOG_FEATURES)
    homolog_embedding = jnp.dot(homolog_reshaped, product_projection, preferred_element_type=jnp.float32).reshape(HOMOLOG_DEPTH, RESIDUE_SPAN, 2 * PRODUCT_FEATURES)
    sequence_live = homolog_present.astype(jnp.float32)
    left_factor = (homolog_embedding[:, :, :PRODUCT_FEATURES] * sequence_live[:, None, None]).astype(jnp.bfloat16)
    right_factor = homolog_embedding[:, :, PRODUCT_FEATURES:].astype(jnp.bfloat16)
    live_count = jnp.sum(sequence_live)
    residue_present = token_live_mask.astype(jnp.float32)
    starts = jnp.arange(RESIDUE_SPAN // TOK_ROW, dtype=jnp.int32) * TOK_ROW

    def pair_block(block_start):
        left_block = lax.dynamic_slice_in_dim(left_factor, block_start, TOK_ROW, 1)
        outer_sum = jnp.einsum('sic,sjd->ijcd', left_block.astype(jnp.float32), right_factor.astype(jnp.float32))
        row_live = lax.dynamic_slice_in_dim(residue_present, block_start, TOK_ROW, 0)
        pair_live = row_live[:, None] * residue_present[None, :]
        mean_scale = pair_live / jnp.maximum(pair_live * live_count, 1.0)
        pair_mean = (outer_sum * mean_scale[:, :, None, None]).astype(jnp.bfloat16).reshape(TOK_ROW * RESIDUE_SPAN, PRODUCT_FEATURES * PRODUCT_FEATURES)
        pair_block_in = lax.dynamic_slice_in_dim(pair_state, block_start, TOK_ROW, 0).reshape(TOK_ROW * RESIDUE_SPAN, CZ)
        pair_mid = (pair_block_in.astype(jnp.float32) + jnp.dot(pair_mean, mean_matrix, preferred_element_type=jnp.float32)).astype(jnp.bfloat16)
        pair_norm = normalized_rows(pair_mid)
        scores = jnp.dot(pair_norm, score_matrix, precision=lax.Precision.HIGHEST, preferred_element_type=jnp.float32)
        hidden_pre = jnp.dot(pair_norm.astype(jnp.bfloat16), transition_input, preferred_element_type=jnp.float32)
        hidden = (jax.nn.silu(hidden_pre[:, :FF]) * hidden_pre[:, FF:]).astype(jnp.bfloat16)
        pair_new = (pair_mid.astype(jnp.float32) + jnp.dot(hidden, transition_output, preferred_element_type=jnp.float32)).astype(jnp.bfloat16)
        return (pair_new.reshape(TOK_ROW, RESIDUE_SPAN, CZ), scores.reshape(TOK_ROW, RESIDUE_SPAN, BLEND_GROUPS))
    pair_output, scores = lax.map(pair_block, starts)
    pair_output = pair_output.reshape(RESIDUE_SPAN, RESIDUE_SPAN, CZ)
    scores = scores.reshape(RESIDUE_SPAN, RESIDUE_SPAN, BLEND_GROUPS)
    row_top = lax.optimization_barrier(jnp.max(scores, axis=1, keepdims=True))
    exp_scores = jnp.exp(scores - row_top)
    blend_coefficients = (exp_scores / lax.optimization_barrier(jnp.sum(exp_scores, axis=1, keepdims=True))).astype(jnp.bfloat16)
    payload_entries = jnp.dot(homolog_reshaped, payload_projection, preferred_element_type=jnp.float32).reshape(HOMOLOG_DEPTH, RESIDUE_SPAN, BLEND_GROUPS * GROUP_FEATURES)
    payload_entries = (payload_entries * residue_present[None, :, None]).astype(jnp.bfloat16).reshape(HOMOLOG_DEPTH, RESIDUE_SPAN, BLEND_GROUPS, GROUP_FEATURES)
    switch_logistic = jax.nn.sigmoid(jnp.dot(homolog_reshaped, switch_projection, preferred_element_type=jnp.float32)).reshape(HOMOLOG_DEPTH, RESIDUE_SPAN, BLEND_GROUPS * GROUP_FEATURES)
    blended_result = jnp.einsum('qfg,rfgn->rqgn', blend_coefficients.astype(jnp.float32), payload_entries.astype(jnp.float32)).reshape(HOMOLOG_DEPTH, RESIDUE_SPAN, BLEND_GROUPS * GROUP_FEATURES)
    switched_blend = (switch_logistic * blended_result).astype(jnp.bfloat16).reshape(HOMOLOG_DEPTH * RESIDUE_SPAN, BLEND_GROUPS * GROUP_FEATURES)
    residue_couple_delta = jnp.dot(switched_blend, return_projection, preferred_element_type=jnp.float32).reshape(HOMOLOG_DEPTH, RESIDUE_SPAN, HOMOLOG_FEATURES)
    alignment_output = (homolog_representation.astype(jnp.float32) + residue_couple_delta).astype(jnp.bfloat16)
    return (alignment_output, pair_output)
```

```python
import functools

import jax
import jax.numpy as jnp
from jax import lax
from jax.experimental import pallas as pl
from jax.experimental.pallas import tpu as pltpu
from jax.sharding import Mesh
from jax.sharding import PartitionSpec as P

F32 = jnp.float32
BF16 = jnp.bfloat16
MESH = pl.DeviceIdType.MESH
epsilon = 1e-05

X, K = 4, 2
SEQ = 8
TOK = 32
ROW = 16
HEADS = 8


def iota(shape, dim):
    return lax.broadcasted_iota(jnp.int32, shape, dim)


def one_hot(condition):
    return jnp.where(condition, 1.0, 0.0).astype(BF16)


def dot(a, b):
    return jnp.dot(a, b, preferred_element_type=F32)


def dot_nt(a, b, precision=None):
    return lax.dot_general(
        a, b, (((1,), (1,)), ((), ())), precision=precision, preferred_element_type=F32
    )


def normalized(source):
    center = source - jnp.mean(source, axis=-1, keepdims=True)
    spread = jnp.mean(center * center, axis=-1, keepdims=True)
    return center * lax.rsqrt(spread + epsilon)


def kernel(
    Y,
    Z,
    h_ref,
    pair_ref,
    seq_ref,
    tok_ref,
    pp_ref,
    mm_ref,
    smt_ref,
    pay_ref,
    sw_ref,
    rett_ref,
    ti_ref,
    to_ref,
    align_ref,
    pout_ref,
    RB,
    LS,
    LX,
    LZ,
    LB,
    HB,
    EY,
    EZ,
    EX,
    MF,
    WB,
    AB,
    VB,
    NB,
    MID,
    PNB,
    ry_s,
    rx_s,
    r_r,
    lx_s,
    lx_r,
    lz_s,
    lz_r,
    ly_s,
    ly_r,
    lk_s,
    hz_s,
    hk_s,
    h_r,
    ey_s,
    ey_r,
    ez_s,
    ez_r,
    ex_s,
    ex_r,
):
    R = Y * X
    C = Z * K
    NS = R * SEQ
    NT = C * TOK
    y, x = lax.axis_index("y"), lax.axis_index("x")
    z, k = lax.axis_index("z"), lax.axis_index("k")
    row = y * X + x
    col = z * K + k
    owner = k == x // 2

    def remote(src, dst, send, recv, **to):
        return pltpu.make_async_remote_copy(
            src_ref=src,
            dst_ref=dst,
            send_sem=send,
            recv_sem=recv,
            device_id=to,
            device_id_type=MESH,
        )

    barrier = pltpu.get_barrier_semaphore()
    for t in range(1, X):
        pl.semaphore_signal(
            barrier, inc=1, device_id={"x": lax.rem(x + t, X)}, device_id_type=MESH
        )
    for t in range(1, Y):
        pl.semaphore_signal(
            barrier, inc=1, device_id={"y": lax.rem(y + t, Y)}, device_id_type=MESH
        )
    for t in range(1, C):
        other = lax.rem(col + t, C)
        pl.semaphore_signal(
            barrier,
            inc=1,
            device_id={"z": other // K, "k": lax.rem(other, K)},
            device_id_type=MESH,
        )

    hf = h_ref[...].reshape(SEQ * TOK, 64).astype(F32)
    norm_f = normalized(hf)
    NB[...] = norm_f.astype(BF16)
    tokens = tok_ref[...].astype(F32)
    seqs = seq_ref[...].astype(F32)
    hit = iota((TOK, NT), 1) == col * TOK + iota((TOK, NT), 0)
    live_tok = jnp.sum(jnp.where(hit, tokens, 0.0), axis=1, keepdims=True)
    live_tok = jnp.concatenate([live_tok] * SEQ, axis=0)
    hit = iota((SEQ * TOK, NS), 1) == row * SEQ + iota((SEQ * TOK, NS), 0) // TOK
    live_seq = jnp.sum(jnp.where(hit, seqs, 0.0), axis=1, keepdims=True)
    inverse_count = 1.0 / jnp.maximum(jnp.sum(seqs, axis=1, keepdims=True), 1.0)
    norm = (norm_f * live_tok).astype(BF16)

    pp = pp_ref[...]
    right_t = dot_nt(one_hot(iota((32, 64), 1) == 32 + iota((32, 64), 0)), pp).astype(BF16)
    spread = []
    for s in range(SEQ):
        one = norm[s * TOK : (s + 1) * TOK]
        spread.append(dot_nt(right_t, jnp.concatenate([one] * 4, axis=0)))
    spread = jnp.concatenate(spread, axis=0)
    mine = iota((256, 128), 0) % 4 == iota((256, 128), 1) // 32
    spread = jnp.where(mine, spread, 0.0).astype(BF16)
    a, b = iota((64, 256), 0), iota((64, 256), 1)
    pick = one_hot((a % 8 == b // 32) & ((b % 32) // 4 == ((a // 8) % 2) * 4 + a // 16))
    packed = dot(pick, spread).astype(BF16)
    for t in range(4):
        RB[row, :, t * 128 : (t + 1) * 128] = packed[t * 16 : (t + 1) * 16]

    left_w = dot(pp, one_hot(iota((64, 128), 0) == iota((64, 128), 1) % 32)).astype(BF16)
    spread = dot(norm, left_w) * live_seq
    spread = jnp.where(mine, spread, 0.0).astype(BF16)
    pick = one_hot(
        (a % 8 == b // 32) & ((b % 32) // 4 == 4 * (a // 32) + 2 * ((a // 8) % 2) + (a // 16) % 2)
    )
    packed = dot(pick, spread).astype(BF16)
    for h in range(2):
        for t in range(2):
            LS[h, :, t * 128 : (t + 1) * 128] = packed[(h * 2 + t) * 16 : (h * 2 + t + 1) * 16]

    u, v = iota((64, 128), 0), iota((64, 128), 1)
    HB[col] = (
        dot(norm[:128], one_hot(u == v)) + dot(norm[128:], one_hot(u + 64 == v))
    ).astype(BF16)

    pl.semaphore_wait(barrier, (X - 1) + (Y - 1) + (C - 1))

    for h in range(2):
        to = 2 * k + h

        @pl.when(to != x)
        def _():
            remote(LS.at[h], LX.at[x], lx_s.at[h], lx_r.at[x], x=to).start()

        @pl.when(to == x)
        def _():
            LX[x] = LS[h]

    def right_y(t):
        return remote(
            RB.at[row], RB.at[row], ry_s.at[t], r_r.at[row], y=lax.rem(y + t, Y)
        )

    def right_x(block, t):
        r = block * X + x
        return remote(
            RB.at[r], RB.at[r], rx_s.at[block, t], r_r.at[r], x=lax.rem(x + t, X)
        )

    def right_arrived(r):
        remote(RB.at[r], RB.at[r], ry_s.at[0], r_r.at[r], x=x).wait_recv()

    for t in range(1, Y):
        right_y(t).start()
    for t in range(1, X):
        right_x(y, t).start()

    MF[...] = mm_ref[...].astype(F32)
    WB[...] = jnp.zeros_like(WB)

    def left_z(t):
        return remote(LZ.at[z], LZ.at[z], lz_s.at[t], lz_r.at[z], z=lax.rem(z + t, Z))

    def hz(t):
        return remote(HB.at[col], HB.at[col], hz_s.at[t], h_r.at[col], z=lax.rem(z + t, Z))

    @pl.when(owner)
    def _():
        for t in range(1, X):
            other = lax.rem(x + t, X)
            remote(LX.at[other], LX.at[other], lx_s.at[0], lx_r.at[other], x=x).wait_recv()
        LZ[z] = LX[...]
        for t in range(1, Z):
            left_z(t).start()

    for t in range(1, Z):
        hz(t).start()

    for d in range(32):
        part = MF[pl.ds(d, 32, stride=32), :].astype(BF16)
        for i in range(4):
            WB[d * 128 + i * 32 : d * 128 + (i + 1) * 32, i * 128 : (i + 1) * 128] = part

    def left_y(block):
        return remote(LZ.at[block], LB.at[y], ly_s.at[block], ly_r.at[y], y=block)

    def left_k(block):
        return remote(LB.at[block], LB.at[block], lk_s.at[block], ly_r.at[block], k=1 - k)

    for t in range(Y):
        if t > 0:
            block = lax.rem(y + Y - t, Y)
            right_arrived(block * X + x)
            for u_ in range(1, X):
                right_x(block, u_).start()
        at = lax.rem(z + Z - t, Z)

        @pl.when(owner)
        def _():
            if t > 0:
                remote(LZ.at[at], LZ.at[at], lz_s.at[0], lz_r.at[at], z=z).wait_recv()

            @pl.when(at != y)
            def _():
                left_y(at).start()

            @pl.when(at == y)
            def _():
                LB[y] = LZ[y]

    @pl.when(owner)
    def _():
        left_k(y).start()
        for t in range(1, Y):
            block = lax.rem(y + Y - t, Y)
            remote(LZ.at[0], LB.at[block], ly_s.at[0], ly_r.at[block], y=y).wait_recv()
            left_k(block).start()

    def hk(block):
        c = block * K + k
        return remote(HB.at[c], HB.at[c], hk_s.at[block], h_r.at[c], k=1 - k)

    def h_arrived(c):
        remote(HB.at[c], HB.at[c], hz_s.at[0], h_r.at[c], z=z).wait_recv()

    hk(z).start()
    for t in range(1, Z):
        block = lax.rem(z + Z - t, Z)
        h_arrived(block * K + k)
        hk(block).start()

    for t in range(1, X):
        other = lax.rem(x + t, X)
        for block in range(Y):
            right_arrived(block * X + other)

    @pl.when(jnp.logical_not(owner))
    def _():
        for block in range(Y):
            remote(LZ.at[0], LB.at[block], ly_s.at[0], ly_r.at[block], y=y).wait_recv()

    left = LB[...].astype(F32).reshape(R, 2, SEQ, 256)
    left = jnp.concatenate(
        [left[:, 0].reshape(NS, 256), left[:, 1].reshape(NS, 256)], axis=1
    ).astype(BF16)
    for half in range(2):
        right = RB[...].astype(F32).reshape(R, 2, SEQ, 512)[:, half].reshape(NS, 512)
        right = jnp.transpose(right).astype(BF16)
        for part in range(2):
            outer = dot(right[part * 256 : (part + 1) * 256], left).astype(BF16)
            for dd in range(8):
                d = half * 16 + part * 8 + dd
                for g in range(4):
                    AB[g * 32 : (g + 1) * 32, d * 128 : (d + 1) * 128] = outer[
                        dd * 32 : (dd + 1) * 32, g * 128 : (g + 1) * 128
                    ]
    mean = dot(AB[...], WB[...]) * inverse_count
    mean = jnp.concatenate(
        [
            mean[(i // 4) * 32 : (i // 4 + 1) * 32, (i % 4) * 128 : (i % 4 + 1) * 128]
            for i in range(ROW)
        ],
        axis=0,
    )
    pair_mid = (pair_ref[...].reshape(ROW * TOK, 128).astype(F32) + mean).astype(BF16)
    MID[...] = pair_mid
    pair_norm = normalized(pair_mid.astype(F32))
    PNB[...] = pair_norm.astype(BF16)
    score_w = jnp.concatenate(
        [jnp.broadcast_to(smt_ref[h : h + 1, :], (ROW, 128)) for h in range(HEADS)], axis=0
    )
    every = dot_nt(pair_norm, score_w, lax.Precision.HIGHEST)
    lane_i = iota((TOK, 128), 1) % ROW
    scores = jnp.zeros((TOK, 128), F32)
    for i in range(ROW):
        scores = jnp.where(lane_i == i, every[i * TOK : (i + 1) * TOK], scores)
    shift = jnp.max(scores, axis=0, keepdims=True).astype(BF16).astype(F32)
    EY[y, 0:TOK, :] = jnp.exp(scores - shift).astype(BF16)
    EY[y, TOK : TOK + 16, :] = jnp.broadcast_to(shift, (16, 128)).astype(BF16)

    def ey(t):
        return remote(EY.at[y], EY.at[y], ey_s.at[t], ey_r.at[y], y=lax.rem(y + t, Y))

    def ez(block):
        return remote(
            EY.at[block], EZ.at[col], ez_s.at[block], ez_r.at[col], z=block, k=x // 2
        )

    def ex(t):
        return remote(
            EX.at[x % 2], EX.at[x % 2], ex_s.at[t], ex_r.at[x % 2], x=lax.rem(x + t, X)
        )

    def forward_z(block):
        away = jnp.logical_or(block != z, jnp.logical_not(owner))

        @pl.when(away)
        def _():
            ez(block).start()

        @pl.when(jnp.logical_not(away))
        def _():
            EZ[col] = EY[z]

    def transition(part):
        rows = slice(part * 128, (part + 1) * 128)
        pre = dot(PNB[rows, :], ti_ref[...])
        gate = pre[:, :512]
        hidden = (gate / (1.0 + jnp.exp(-gate)) * pre[:, 512:]).astype(BF16)
        out = (MID[rows, :].astype(F32) + dot(hidden, to_ref[...])).astype(BF16)
        pout_ref[part * 4 : (part + 1) * 4] = out.reshape(4, TOK, 128)

    for t in range(1, Y):
        ey(t).start()
    forward_z(y)
    transition(0)
    for t in range(1, Y):
        block = lax.rem(y + Y - t, Y)
        remote(EY.at[block], EY.at[block], ey_s.at[0], ey_r.at[block], y=y).wait_recv()
        forward_z(block)
    transition(1)
    transition(2)

    @pl.when(owner)
    def _():
        for t in range(1, C):
            c = lax.rem(col + t, C)
            remote(EY.at[0], EZ.at[c], ez_s.at[0], ez_r.at[c], z=z).wait_recv()
        shifts = EZ[:, TOK : TOK + 16, :].astype(F32)[:, 0:1, :]
        factor = jnp.exp(shifts - jnp.max(shifts, axis=0, keepdims=True))
        weights = EZ[:, 0:TOK, :].astype(F32) * factor
        total = jnp.sum(jnp.sum(weights, axis=0, keepdims=True), axis=1, keepdims=True)
        EX[x % 2] = (weights / total).astype(BF16).reshape(NT, 128)
        for t in range(1, X):
            ex(t).start()

    transition(3)

    for t in range(Z):
        h_arrived(t * K + 1 - k)
    zeros = jnp.zeros((64, 256), BF16)
    for side in range(2):
        pay = jnp.concatenate(
            [pay_ref[...], zeros] if side == 0 else [zeros, pay_ref[...]], axis=0
        )
        for s in range(4):
            rows = HB[:, s * TOK : (s + 1) * TOK, :].reshape(NT, 128)
            VB[side * 4 + s] = dot(rows, pay).astype(BF16)
    gate = jax.nn.sigmoid(dot(NB[...], sw_ref[...]))

    for h in range(2):

        @pl.when(x != 2 * k + h)
        def _():
            remote(EX.at[h], EX.at[h], ex_s.at[0], ex_r.at[h], x=x).wait_recv()

    weights = jnp.concatenate(
        [jnp.transpose(EX[h].astype(F32)).astype(BF16) for h in range(2)], axis=0
    )
    head = iota((ROW, 256), 1) // 32
    averages = []
    for s in range(SEQ):
        full = dot(weights, VB[s])
        for half in range(2):
            average = jnp.zeros((ROW, 256), F32)
            for g in range(HEADS):
                start = half * 128 + g * ROW
                average = jnp.where(head == g, full[start : start + ROW], average)
            averages.append(average)
    gated = (gate * jnp.concatenate(averages, axis=0)).astype(BF16)
    out = h_ref[...].reshape(SEQ * TOK, 64).astype(F32) + dot_nt(gated, rett_ref[...])
    align_ref[...] = out.astype(BF16).reshape(SEQ, TOK, 64)

    for h in range(2):

        @pl.when(2 * k + h != x)
        def _():
            remote(LS.at[h], LX.at[x], lx_s.at[h], lx_r.at[x], x=2 * k + h).wait_send()

    for t in range(1, Y):
        right_y(t).wait_send()
        ey(t).wait_send()
    for block in range(Y):
        for t in range(1, X):
            right_x(block, t).wait_send()
    for t in range(1, Z):
        hz(t).wait_send()
    for block in range(Z):
        hk(block).wait_send()

        @pl.when(jnp.logical_or(block != z, jnp.logical_not(owner)))
        def _():
            ez(block).wait_send()

    @pl.when(owner)
    def _():
        for t in range(1, Z):
            left_z(t).wait_send()
        for block in range(Z):

            @pl.when(block != y)
            def _():
                left_y(block).wait_send()

            left_k(block).wait_send()
        for t in range(1, X):
            ex(t).wait_send()


def body(h, pair, seq, tok, pp, mm, sm, pay, sw, ret, ti, to, *, Y, Z):
    R, C = Y * X, Z * K
    NT = C * TOK
    dma = pltpu.SemaphoreType.DMA
    vmem = pl.BlockSpec(memory_space=pltpu.VMEM)
    return pl.pallas_call(
        functools.partial(kernel, Y, Z),
        out_shape=(
            jax.ShapeDtypeStruct(h.shape, BF16),
            jax.ShapeDtypeStruct(pair.shape, BF16),
        ),
        in_specs=[vmem] * 12,
        out_specs=(vmem, vmem),
        scratch_shapes=[
            pltpu.VMEM((R, 16, 512), BF16),
            pltpu.VMEM((2, 16, 256), BF16),
            pltpu.VMEM((X, 16, 256), BF16),
            pltpu.VMEM((Z, X, 16, 256), BF16),
            pltpu.VMEM((Y, X, 16, 256), BF16),
            pltpu.VMEM((C, 128, 128), BF16),
            pltpu.VMEM((Y, TOK + 16, 128), BF16),
            pltpu.VMEM((C, TOK + 16, 128), BF16),
            pltpu.VMEM((2, NT, 128), BF16),
            pltpu.VMEM((1024, 128), F32),
            pltpu.VMEM((4096, 512), BF16),
            pltpu.VMEM((128, 4096), BF16),
            pltpu.VMEM((SEQ, NT, 256), BF16),
            pltpu.VMEM((256, 64), BF16),
            pltpu.VMEM((512, 128), BF16),
            pltpu.VMEM((512, 128), BF16),
            dma((Y,)),
            dma((Y, X)),
            dma((R,)),
            dma((2,)),
            dma((X,)),
            dma((Z,)),
            dma((Z,)),
            dma((Z,)),
            dma((Y,)),
            dma((Y,)),
            dma((Z,)),
            dma((Z,)),
            dma((C,)),
            dma((Y,)),
            dma((Y,)),
            dma((Z,)),
            dma((C,)),
            dma((X,)),
            dma((2,)),
        ],
        compiler_params=pltpu.CompilerParams(
            collective_id=0, has_side_effects=True, vmem_limit_bytes=48 * 1024 * 1024
        ),
        cost_estimate=pl.CostEstimate(
            flops=3_000_000_000, bytes_accessed=2_000_000, transcendentals=400_000
        ),
    )(h, pair, seq.reshape(1, -1), tok.reshape(1, -1), pp, mm, sm.T, pay, sw, ret.T, ti, to)


def solution(mesh):
    Y, Z = mesh.shape["row"] // X, mesh.shape["col"] // K
    split = Mesh(mesh.devices.reshape(Y, X, Z, K), ("y", "x", "z", "k"))
    tiled = P(("y", "x"), ("z", "k"), None)
    return jax.shard_map(
        functools.partial(body, Y=Y, Z=Z),
        mesh=split,
        in_specs=(tiled, tiled) + (P(),) * 10,
        out_specs=(tiled, tiled),
        check_vma=False,
    )
```

```python
import functools

import jax
import jax.numpy as jnp
from jax import lax
from jax.experimental import pallas as pl
from jax.experimental.pallas import tpu as pltpu
from jax.sharding import Mesh
from jax.sharding import PartitionSpec as P

F32 = jnp.float32
BF16 = jnp.bfloat16
MESH = pl.DeviceIdType.MESH
epsilon = 1e-05

X, K = 4, 2
SEQ = 8
TOK = 32
ROW = 16
HEADS = 8


def iota(shape, dim):
    return lax.broadcasted_iota(jnp.int32, shape, dim)


def one_hot(condition):
    return jnp.where(condition, 1.0, 0.0).astype(BF16)


def dot(a, b):
    return jnp.dot(a, b, preferred_element_type=F32)


def dot_nt(a, b, precision=None):
    return lax.dot_general(
        a, b, (((1,), (1,)), ((), ())), precision=precision, preferred_element_type=F32
    )


def normalized(source):
    center = source - jnp.mean(source, axis=-1, keepdims=True)
    spread = jnp.mean(center * center, axis=-1, keepdims=True)
    return center * lax.rsqrt(spread + epsilon)


def kernel(Y, Z, *refs):
    R = Y * X
    C = Z * K
    NS = R * SEQ
    NT = C * TOK
    hbm, (align_ref, pout_ref), refs = refs[:12], refs[12:14], refs[14:]
    local, refs = refs[:12], refs[12:]
    h_ref, pair_ref, seq_ref, tok_ref, pp_ref, mm_ref = local[:6]
    smt_ref, pay_ref, sw_ref, rett_ref, ti_ref, to_ref = local[6:]
    RB, LZ, LB, HB, EY, EX, MF, WB, AB, RT, VB, NB, MID, PNB = refs[:14]
    in_s, ry_s, rx_s, r_r, lz_s, lz_r, lx_s, l_r, lk_s, lk_r = refs[14:24]
    hz_s, hk_s, h_r, ez_s, ez_r, ex_s, ex_r = refs[24:]
    y, x = lax.axis_index("y"), lax.axis_index("x")
    z, k = lax.axis_index("z"), lax.axis_index("k")
    row = y * X + x
    col = z * K + k
    owner = k == x // 2
    far_first = sorted(range(1, Z), key=lambda t: -min(t, Z - t))
    near_first = far_first[::-1]

    def remote(src, dst, send, recv, **to):
        return pltpu.make_async_remote_copy(
            src_ref=src,
            dst_ref=dst,
            send_sem=send,
            recv_sem=recv,
            device_id=to,
            device_id_type=MESH,
        )

    barrier = pltpu.get_barrier_semaphore()
    for t in range(1, R):
        other = lax.rem(row + t, R)
        pl.semaphore_signal(
            barrier,
            inc=1,
            device_id={"y": other // X, "x": lax.rem(other, X)},
            device_id_type=MESH,
        )
    for t in range(1, C):
        other = lax.rem(col + t, C)
        pl.semaphore_signal(
            barrier,
            inc=1,
            device_id={"z": other // K, "k": lax.rem(other, K)},
            device_id_type=MESH,
        )

    def fetch(i):
        return pltpu.make_async_copy(hbm[i], local[i], in_s.at[i])

    for i in (0, 4, 3, 2, 5, 1, 6, 10, 11, 7, 8, 9):
        fetch(i).start()
    for i in (0, 4, 3, 2):
        fetch(i).wait()

    hf = h_ref[...].reshape(SEQ * TOK, 64).astype(F32)
    norm_f = normalized(hf)
    NB[...] = norm_f.astype(BF16)
    tokens = tok_ref[...].astype(F32)
    seqs = seq_ref[...].astype(F32)
    hit = iota((TOK, NT), 1) == col * TOK + iota((TOK, NT), 0)
    live_tok = jnp.sum(jnp.where(hit, tokens, 0.0), axis=1, keepdims=True)
    live_tok = jnp.concatenate([live_tok] * SEQ, axis=0)
    hit = iota((SEQ * TOK, NS), 1) == row * SEQ + iota((SEQ * TOK, NS), 0) // TOK
    live_seq = jnp.sum(jnp.where(hit, seqs, 0.0), axis=1, keepdims=True)
    inverse_count = 1.0 / jnp.maximum(jnp.sum(seqs, axis=1, keepdims=True), 1.0)
    norm = (norm_f * live_tok).astype(BF16)

    pp = pp_ref[...]
    mine = iota((256, 128), 0) % 4 == iota((256, 128), 1) // 32
    a, b = iota((64, 256), 0), iota((64, 256), 1)
    left_w = dot(pp, one_hot(iota((64, 128), 0) == iota((64, 128), 1) % 32)).astype(BF16)
    spread = dot(norm, left_w) * live_seq
    spread = jnp.where(mine, spread, 0.0).astype(BF16)
    pick = one_hot(
        (a % 8 == b // 32) & ((b % 32) // 4 == 4 * (a // 32) + 2 * ((a // 8) % 2) + (a // 16) % 2)
    )
    packed = dot(pick, spread).astype(BF16)
    for h in range(2):
        for t in range(2):
            LZ[z, h, :, t * 128 : (t + 1) * 128] = packed[(h * 2 + t) * 16 : (h * 2 + t + 1) * 16]

    right_t = dot_nt(one_hot(iota((32, 64), 1) == 32 + iota((32, 64), 0)), pp).astype(BF16)
    spread = []
    for s in range(SEQ):
        one = norm[s * TOK : (s + 1) * TOK]
        spread.append(dot_nt(right_t, jnp.concatenate([one] * 4, axis=0)))
    spread = jnp.concatenate(spread, axis=0)
    spread = jnp.where(mine, spread, 0.0).astype(BF16)
    pick = one_hot((a % 8 == b // 32) & ((b % 32) // 4 == ((a // 8) % 2) * 4 + a // 16))
    packed = dot(pick, spread).astype(BF16)
    for t in range(4):
        RB[row, :, t * 128 : (t + 1) * 128] = packed[t * 16 : (t + 1) * 16]

    u, v = iota((64, 128), 0), iota((64, 128), 1)
    HB[col] = (
        dot(norm[:128], one_hot(u == v)) + dot(norm[128:], one_hot(u + 64 == v))
    ).astype(BF16)

    pl.semaphore_wait(barrier, (R - 1) + (C - 1))

    def left_z(t):
        return remote(LZ.at[z], LZ.at[z], lz_s.at[t], lz_r.at[z], z=lax.rem(z + t, Z))

    def left_x(block, h):
        return remote(
            LZ.at[block, h],
            LB.at[row],
            lx_s.at[block, h],
            l_r.at[row],
            y=block,
            x=2 * k + h,
        )

    def left_here(block, h):
        return jnp.logical_and(block == y, 2 * k + h == x)

    def left_forward(block):
        for h in range(2):

            @pl.when(jnp.logical_not(left_here(block, h)))
            def _():
                left_x(block, h).start()

            @pl.when(left_here(block, h))
            def _():
                LB[row] = LZ[block, h]

    def left_k(block):
        part = pl.ds(block * X, X)
        return remote(LB.at[part], LB.at[part], lk_s.at[block], lk_r.at[block], k=1 - k)

    def right_y(t):
        return remote(RB.at[row], RB.at[row], ry_s.at[t], r_r.at[row], y=lax.rem(y + t, Y))

    def right_x(block, t):
        r = block * X + x
        return remote(
            RB.at[r], RB.at[r], rx_s.at[block, t], r_r.at[r], x=lax.rem(x + t, X)
        )

    def right_arrived(r):
        remote(RB.at[r], RB.at[r], ry_s.at[0], r_r.at[r], x=x).wait_recv()

    for t in far_first:
        left_z(t).start()
    for t in far_first:
        right_y(t).start()
    left_forward(z)
    for t in (2, 1, 3):
        right_x(y, t).start()

    fetch(5).wait()
    MF[...] = mm_ref[...].astype(F32)
    WB[...] = jnp.zeros_like(WB)
    for d in range(32):
        part = MF[pl.ds(d, 32, stride=32), :].astype(BF16)
        for i in range(4):
            WB[d * 128 + i * 32 : d * 128 + (i + 1) * 32, i * 128 : (i + 1) * 128] = part

    todo = list(near_first)
    for block in range(Y):

        @pl.when(block != y)
        def _():
            right_arrived(block * X + x)
            for t in (2, 1, 3):
                right_x(block, t).start()

        for t in todo[:2]:
            at = lax.rem(z + t, Z)
            remote(LZ.at[at], LZ.at[at], lz_s.at[0], lz_r.at[at], z=z).wait_recv()
            left_forward(at)
        todo = todo[2:]

    def hz(t):
        return remote(HB.at[col], HB.at[col], hz_s.at[t], h_r.at[col], z=lax.rem(z + t, Z))

    def hk(block):
        c = block * K + k
        return remote(HB.at[c], HB.at[c], hk_s.at[block], h_r.at[c], k=1 - k)

    def h_arrived(c):
        remote(HB.at[c], HB.at[c], hz_s.at[0], h_r.at[c], z=z).wait_recv()

    for t in far_first:
        hz(t).start()

    @pl.when(owner)
    def _():
        for block in range(Y):
            for other in range(X):
                r = block * X + other

                @pl.when(r != row)
                def _():
                    remote(LB.at[r], LB.at[r], lx_s.at[0, 0], l_r.at[r], x=x).wait_recv()

            left_k(block).start()

    for block in range(Y):
        for t in range(1, X):
            right_arrived(block * X + lax.rem(x + t, X))
    for half in range(2):
        right = RB[...].astype(F32).reshape(R, 2, SEQ, 512)[:, half].reshape(NS, 512)
        RT[half * 512 : (half + 1) * 512, :] = jnp.transpose(right).astype(BF16)

    @pl.when(jnp.logical_not(owner))
    def _():
        for block in range(Y):
            part = pl.ds(block * X, X)
            remote(LB.at[part], LB.at[part], lk_s.at[0], lk_r.at[block], y=y).wait_recv()

    left = LB[...].astype(F32).reshape(R, 2, SEQ, 256)
    left = jnp.concatenate(
        [left[:, 0].reshape(NS, 256), left[:, 1].reshape(NS, 256)], axis=1
    ).astype(BF16)
    for part in range(4):
        outer = dot(RT[part * 256 : (part + 1) * 256, :], left).astype(BF16)
        for dd in range(8):
            d = part * 8 + dd
            for g in range(4):
                AB[g * 32 : (g + 1) * 32, d * 128 : (d + 1) * 128] = outer[
                    dd * 32 : (dd + 1) * 32, g * 128 : (g + 1) * 128
                ]
    mean = dot(AB[...], WB[...]) * inverse_count
    mean = jnp.concatenate(
        [
            mean[(i // 4) * 32 : (i // 4 + 1) * 32, (i % 4) * 128 : (i % 4 + 1) * 128]
            for i in range(ROW)
        ],
        axis=0,
    )
    fetch(1).wait()
    fetch(6).wait()
    pair_mid = (pair_ref[...].reshape(ROW * TOK, 128).astype(F32) + mean).astype(BF16)
    MID[...] = pair_mid
    pair_norm = normalized(pair_mid.astype(F32))
    PNB[...] = pair_norm.astype(BF16)
    score_w = jnp.concatenate(
        [jnp.broadcast_to(smt_ref[h : h + 1, :], (ROW, 128)) for h in range(HEADS)], axis=0
    )
    every = dot_nt(pair_norm, score_w, lax.Precision.HIGHEST)
    lane_i = iota((TOK, 128), 1) % ROW
    scores = jnp.zeros((TOK, 128), F32)
    for i in range(ROW):
        scores = jnp.where(lane_i == i, every[i * TOK : (i + 1) * TOK], scores)
    shift = jnp.max(scores, axis=0, keepdims=True).astype(BF16).astype(F32)
    EY[0:TOK, :] = jnp.exp(scores - shift).astype(BF16)
    EY[TOK : TOK + 16, :] = jnp.broadcast_to(shift, (16, 128)).astype(BF16)

    def ez(to):
        return remote(
            EY, EX.at[x % 2, col], ez_s.at[to], ez_r.at[col], y=to, z=y, k=x // 2
        )

    def e_here(to):
        return jnp.logical_and(jnp.logical_and(to == y, z == y), owner)

    def ex(block, t):
        part = pl.ds(block * K, K)
        return remote(
            EX.at[x % 2, part],
            EX.at[x % 2, part],
            ex_s.at[block, t],
            ex_r.at[x % 2, block],
            x=lax.rem(x + t, X),
        )

    for to in range(Y):

        @pl.when(jnp.logical_not(e_here(to)))
        def _():
            ez(to).start()

        @pl.when(e_here(to))
        def _():
            EX[x % 2, col] = EY[...]

    hk(z).start()
    for t in near_first:
        block = lax.rem(z + t, Z)
        h_arrived(block * K + k)
        hk(block).start()
    fetch(10).wait()
    fetch(11).wait()
    for part in range(4):
        rows = slice(part * 128, (part + 1) * 128)
        pre = dot(PNB[rows, :], ti_ref[...])
        gate = pre[:, :512]
        hidden = (gate / (1.0 + jnp.exp(-gate)) * pre[:, 512:]).astype(BF16)
        out = (MID[rows, :].astype(F32) + dot(hidden, to_ref[...])).astype(BF16)
        pout_ref[part * 4 : (part + 1) * 4] = out.reshape(4, TOK, 128)

    @pl.when(owner)
    def _():
        for block in range(Z):
            for j in range(K):
                c = block * K + j

                @pl.when(jnp.logical_or(c != col, y != z))
                def _():
                    remote(EY, EX.at[x % 2, c], ez_s.at[0], ez_r.at[c], z=z).wait_recv()

            for t in (2, 1, 3):
                ex(block, t).start()

    for i in (7, 8, 9):
        fetch(i).wait()
    for t in range(Z):
        h_arrived(t * K + 1 - k)
    zeros = jnp.zeros((64, 256), BF16)
    for side in range(2):
        pay = jnp.concatenate(
            [pay_ref[...], zeros] if side == 0 else [zeros, pay_ref[...]], axis=0
        )
        for s in range(4):
            rows = HB[:, s * TOK : (s + 1) * TOK, :].reshape(NT, 128)
            VB[side * 4 + s] = dot(rows, pay).astype(BF16)
    gate = jax.nn.sigmoid(dot(NB[...], sw_ref[...]))

    weights = []
    for h in range(2):

        @pl.when(x != 2 * k + h)
        def _():
            for block in range(Z):
                part = pl.ds(block * K, K)
                remote(
                    EX.at[h, part], EX.at[h, part], ex_s.at[0, 0], ex_r.at[h, block], x=x
                ).wait_recv()

        shifts = EX[h, :, TOK : TOK + 16, :].astype(F32)[:, 0:1, :]
        factor = jnp.exp(shifts - jnp.max(shifts, axis=0, keepdims=True))
        w = EX[h, :, 0:TOK, :].astype(F32) * factor
        total = jnp.sum(jnp.sum(w, axis=0, keepdims=True), axis=1, keepdims=True)
        weights.append(jnp.transpose((w / total).reshape(NT, 128)).astype(BF16))
    weights = jnp.concatenate(weights, axis=0)
    head = iota((ROW, 256), 1) // 32
    averages = []
    for s in range(SEQ):
        full = dot(weights, VB[s])
        for half in range(2):
            average = jnp.zeros((ROW, 256), F32)
            for g in range(HEADS):
                start = half * 128 + g * ROW
                average = jnp.where(head == g, full[start : start + ROW], average)
            averages.append(average)
    gated = (gate * jnp.concatenate(averages, axis=0)).astype(BF16)
    out = h_ref[...].reshape(SEQ * TOK, 64).astype(F32) + dot_nt(gated, rett_ref[...])
    align_ref[...] = out.astype(BF16).reshape(SEQ, TOK, 64)

    for t in range(1, Y):
        right_y(t).wait_send()
    for block in range(Y):
        for t in range(1, X):
            right_x(block, t).wait_send()

        @pl.when(jnp.logical_not(e_here(block)))
        def _():
            ez(block).wait_send()

    for t in range(1, Z):
        left_z(t).wait_send()
        hz(t).wait_send()
    for block in range(Z):
        hk(block).wait_send()
        for h in range(2):

            @pl.when(jnp.logical_not(left_here(block, h)))
            def _():
                left_x(block, h).wait_send()

    @pl.when(owner)
    def _():
        for block in range(Y):
            left_k(block).wait_send()
        for block in range(Z):
            for t in range(1, X):
                ex(block, t).wait_send()


def body(h, pair, seq, tok, pp, mm, sm, pay, sw, ret, ti, to, *, Y, Z):
    R, C = Y * X, Z * K
    NT = C * TOK
    dma = pltpu.SemaphoreType.DMA
    args = (h, pair, seq.reshape(1, -1), tok.reshape(1, -1), pp, mm)
    args += (sm.T, pay, sw, ret.T, ti, to)
    return pl.pallas_call(
        functools.partial(kernel, Y, Z),
        out_shape=(
            jax.ShapeDtypeStruct(h.shape, BF16),
            jax.ShapeDtypeStruct(pair.shape, BF16),
        ),
        in_specs=[pl.BlockSpec(memory_space=pl.ANY)] * 12,
        out_specs=(pl.BlockSpec(memory_space=pltpu.VMEM),) * 2,
        scratch_shapes=[pltpu.VMEM(v.shape, v.dtype) for v in args]
        + [
            pltpu.VMEM((R, 16, 512), BF16),
            pltpu.VMEM((Z, 2, 16, 256), BF16),
            pltpu.VMEM((R, 16, 256), BF16),
            pltpu.VMEM((C, 128, 128), BF16),
            pltpu.VMEM((TOK + 16, 128), BF16),
            pltpu.VMEM((2, C, TOK + 16, 128), BF16),
            pltpu.VMEM((1024, 128), F32),
            pltpu.VMEM((4096, 512), BF16),
            pltpu.VMEM((128, 4096), BF16),
            pltpu.VMEM((1024, R * SEQ), BF16),
            pltpu.VMEM((SEQ, NT, 256), BF16),
            pltpu.VMEM((256, 64), BF16),
            pltpu.VMEM((512, 128), BF16),
            pltpu.VMEM((512, 128), BF16),
            dma((12,)),
            dma((Y,)),
            dma((Y, X)),
            dma((R,)),
            dma((Z,)),
            dma((Z,)),
            dma((Z, 2)),
            dma((R,)),
            dma((Y,)),
            dma((Y,)),
            dma((Z,)),
            dma((Z,)),
            dma((C,)),
            dma((Y,)),
            dma((C,)),
            dma((Z, X)),
            dma((2, Z)),
        ],
        compiler_params=pltpu.CompilerParams(
            collective_id=0, has_side_effects=True, vmem_limit_bytes=56 * 1024 * 1024
        ),
        cost_estimate=pl.CostEstimate(
            flops=3_000_000_000, bytes_accessed=2_000_000, transcendentals=400_000
        ),
    )(*args)


def solution(mesh):
    Y, Z = mesh.shape["row"] // X, mesh.shape["col"] // K
    split = Mesh(mesh.devices.reshape(Y, X, Z, K), ("y", "x", "z", "k"))
    tiled = P(("y", "x"), ("z", "k"), None)
    return jax.shard_map(
        functools.partial(body, Y=Y, Z=Z),
        mesh=split,
        in_specs=(tiled, tiled) + (P(),) * 10,
        out_specs=(tiled, tiled),
        check_vma=False,
    )
```

```python
import functools

import jax
import jax.numpy as jnp
from jax import lax
from jax.experimental import pallas as pl
from jax.experimental.pallas import tpu as pltpu
from jax.sharding import Mesh
from jax.sharding import PartitionSpec as P

F32 = jnp.float32
BF16 = jnp.bfloat16
MESH = pl.DeviceIdType.MESH
epsilon = 1e-05

X, K = 4, 2
SEQ = 8
TOK = 32
ROW = 16
HEADS = 8


def iota(shape, dim):
    return lax.broadcasted_iota(jnp.int32, shape, dim)


def one_hot(condition):
    return jnp.where(condition, 1.0, 0.0).astype(BF16)


def dot(a, b):
    return jnp.dot(a, b, preferred_element_type=F32)


def dot_nt(a, b, precision=None):
    return lax.dot_general(
        a, b, (((1,), (1,)), ((), ())), precision=precision, preferred_element_type=F32
    )


def normalized(source):
    center = source - jnp.mean(source, axis=-1, keepdims=True)
    spread = jnp.mean(center * center, axis=-1, keepdims=True)
    return center * lax.rsqrt(spread + epsilon)


def kernel(Y, Z, *refs):
    R = Y * X
    C = Z * K
    NS = R * SEQ
    NT = C * TOK
    hbm, (align_ref, pout_ref), refs = refs[:12], refs[12:14], refs[14:]
    local, refs = refs[:12], refs[12:]
    h_ref, pair_ref, seq_ref, tok_ref, pp_ref, mm_ref = local[:6]
    smt_ref, pay_ref, sw_ref, rett_ref, ti_ref, to_ref = local[6:]
    RB, LZ, LB, HB, EY, EX, MF, WB, AB, RT, VB, NB, MID, PNB = refs[:14]
    in_s, ry_s, rx_s, r_r, lz_s, lz_r, lx_s, l_r, lk_s, lk_r = refs[14:24]
    hz_s, hk_s, h_r, ez_s, ez_r, ex_s, ex_r = refs[24:]
    y, x = lax.axis_index("y"), lax.axis_index("x")
    z, k = lax.axis_index("z"), lax.axis_index("k")
    row = y * X + x
    col = z * K + k
    owner = k == x // 2
    far_first = sorted(range(1, Z), key=lambda t: -min(t, Z - t))
    near_first = far_first[::-1]

    def remote(src, dst, send, recv, **to):
        return pltpu.make_async_remote_copy(
            src_ref=src,
            dst_ref=dst,
            send_sem=send,
            recv_sem=recv,
            device_id=to,
            device_id_type=MESH,
        )

    barrier = pltpu.get_barrier_semaphore()
    for axis, at, size in (("y", y, Y), ("x", x, X)):
        for t in range(1, size):
            pl.semaphore_signal(
                barrier, inc=1, device_id={axis: lax.rem(at + t, size)}, device_id_type=MESH
            )
    for t in range(1, C):
        other = lax.rem(col + t, C)
        pl.semaphore_signal(
            barrier,
            inc=1,
            device_id={"z": other // K, "k": lax.rem(other, K)},
            device_id_type=MESH,
        )

    def fetch(i):
        return pltpu.make_async_copy(hbm[i], local[i], in_s.at[i])

    for i in (0, 4, 3, 2, 5, 1, 6, 10, 11, 7, 8, 9):
        fetch(i).start()
    for i in (0, 4, 3, 2):
        fetch(i).wait()

    hf = h_ref[...].reshape(SEQ * TOK, 64).astype(F32)
    norm_f = normalized(hf)
    NB[...] = norm_f.astype(BF16)
    tokens = tok_ref[...].astype(F32)
    seqs = seq_ref[...].astype(F32)
    hit = iota((TOK, NT), 1) == col * TOK + iota((TOK, NT), 0)
    live_tok = jnp.sum(jnp.where(hit, tokens, 0.0), axis=1, keepdims=True)
    live_tok = jnp.concatenate([live_tok] * SEQ, axis=0)
    hit = iota((SEQ * TOK, NS), 1) == row * SEQ + iota((SEQ * TOK, NS), 0) // TOK
    live_seq = jnp.sum(jnp.where(hit, seqs, 0.0), axis=1, keepdims=True)
    inverse_count = 1.0 / jnp.maximum(jnp.sum(seqs, axis=1, keepdims=True), 1.0)
    norm = (norm_f * live_tok).astype(BF16)

    pp = pp_ref[...]
    mine = iota((256, 128), 0) % 4 == iota((256, 128), 1) // 32
    a, b = iota((64, 256), 0), iota((64, 256), 1)
    left_w = dot(pp, one_hot(iota((64, 128), 0) == iota((64, 128), 1) % 32)).astype(BF16)
    spread = dot(norm, left_w) * live_seq
    spread = jnp.where(mine, spread, 0.0).astype(BF16)
    pick = one_hot(
        (a % 8 == b // 32) & ((b % 32) // 4 == 4 * (a // 32) + 2 * ((a // 8) % 2) + (a // 16) % 2)
    )
    packed = dot(pick, spread).astype(BF16)
    for h in range(2):
        for t in range(2):
            LZ[z, h, :, t * 128 : (t + 1) * 128] = packed[(h * 2 + t) * 16 : (h * 2 + t + 1) * 16]

    right_t = dot_nt(one_hot(iota((32, 64), 1) == 32 + iota((32, 64), 0)), pp).astype(BF16)
    spread = []
    for s in range(SEQ):
        one = norm[s * TOK : (s + 1) * TOK]
        spread.append(dot_nt(right_t, jnp.concatenate([one] * 4, axis=0)))
    spread = jnp.concatenate(spread, axis=0)
    spread = jnp.where(mine, spread, 0.0).astype(BF16)
    pick = one_hot((a % 8 == b // 32) & ((b % 32) // 4 == ((a // 8) % 2) * 4 + a // 16))
    packed = dot(pick, spread).astype(BF16)
    for t in range(4):
        RB[row, :, t * 128 : (t + 1) * 128] = packed[t * 16 : (t + 1) * 16]

    pl.semaphore_wait(barrier, (Y - 1) + (X - 1) + (C - 1))

    def left_z(t):
        return remote(LZ.at[z], LZ.at[z], lz_s.at[t], lz_r.at[z], z=lax.rem(z + t, Z))

    def left_x(block, h):
        return remote(
            LZ.at[block, h],
            LB.at[row],
            lx_s.at[block, h],
            l_r.at[row],
            y=block,
            x=2 * k + h,
        )

    def left_here(block, h):
        return jnp.logical_and(block == y, 2 * k + h == x)

    def left_forward(block):
        for h in range(2):

            @pl.when(jnp.logical_not(left_here(block, h)))
            def _():
                left_x(block, h).start()

            @pl.when(left_here(block, h))
            def _():
                LB[row] = LZ[block, h]

    def left_k(block):
        part = pl.ds(block * X, X)
        return remote(LB.at[part], LB.at[part], lk_s.at[block], lk_r.at[block], k=1 - k)

    def right_y(t):
        return remote(RB.at[row], RB.at[row], ry_s.at[t], r_r.at[row], y=lax.rem(y + t, Y))

    def right_x(block, t):
        r = block * X + x
        return remote(
            RB.at[r], RB.at[r], rx_s.at[block, t], r_r.at[r], x=lax.rem(x + t, X)
        )

    def right_arrived(r):
        remote(RB.at[r], RB.at[r], ry_s.at[0], r_r.at[r], x=x).wait_recv()

    for t in far_first:
        left_z(t).start()
    for t in far_first:
        right_y(t).start()
    for t in (2, 1, 3):
        right_x(y, t).start()

    u, v = iota((64, 128), 0), iota((64, 128), 1)
    HB[col] = (
        dot(norm[:128], one_hot(u == v)) + dot(norm[128:], one_hot(u + 64 == v))
    ).astype(BF16)

    fetch(5).wait()
    MF[...] = mm_ref[...].astype(F32)
    WB[...] = jnp.zeros_like(WB)
    for d in range(32):
        part = MF[pl.ds(d, 32, stride=32), :].astype(BF16)
        for i in range(4):
            WB[d * 128 + i * 32 : d * 128 + (i + 1) * 32, i * 128 : (i + 1) * 128] = part

    half = Y // 2
    outer = jnp.logical_or(z < Y // 4, z >= Y - Y // 4)

    def right_forward(block):
        @pl.when(block != y)
        def _():
            right_arrived(block * X + x)
            for t in (2, 1, 3):
                right_x(block, t).start()

    def left_next(block):
        @pl.when(block != z)
        def _():
            remote(
                LZ.at[block], LZ.at[block], lz_s.at[0], lz_r.at[block], z=z
            ).wait_recv()

        left_forward(block)

    for i in range(half):
        right_forward(i)
    for i in range(half):
        left_next(jnp.where(outer, i, half - 1 - i))
    for i in range(half, Y):
        block = jnp.where(outer, Y + half - 1 - i, i)
        right_forward(block)
        left_next(block)

    def hz(t):
        return remote(HB.at[col], HB.at[col], hz_s.at[t], h_r.at[col], z=lax.rem(z + t, Z))

    def hk(block):
        c = block * K + k
        return remote(HB.at[c], HB.at[c], hk_s.at[block], h_r.at[c], k=1 - k)

    def h_arrived(c):
        remote(HB.at[c], HB.at[c], hz_s.at[0], h_r.at[c], z=z).wait_recv()

    for t in far_first:
        hz(t).start()

    @pl.when(owner)
    def _():
        for block in range(Y):
            for other in range(X):
                r = block * X + other

                @pl.when(r != row)
                def _():
                    remote(LB.at[r], LB.at[r], lx_s.at[0, 0], l_r.at[r], x=x).wait_recv()

            left_k(block).start()

    for block in range(Y):
        for t in range(1, X):
            right_arrived(block * X + lax.rem(x + t, X))
    for half in range(2):
        right = RB[...].astype(F32).reshape(R, 2, SEQ, 512)[:, half].reshape(NS, 512)
        RT[half * 512 : (half + 1) * 512, :] = jnp.transpose(right).astype(BF16)

    @pl.when(jnp.logical_not(owner))
    def _():
        for block in range(Y):
            part = pl.ds(block * X, X)
            remote(LB.at[part], LB.at[part], lk_s.at[0], lk_r.at[block], y=y).wait_recv()

    left = LB[...].astype(F32).reshape(R, 2, SEQ, 256)
    left = jnp.concatenate(
        [left[:, 0].reshape(NS, 256), left[:, 1].reshape(NS, 256)], axis=1
    ).astype(BF16)
    for part in range(4):
        outer = dot(RT[part * 256 : (part + 1) * 256, :], left).astype(BF16)
        for dd in range(8):
            d = part * 8 + dd
            for g in range(4):
                AB[g * 32 : (g + 1) * 32, d * 128 : (d + 1) * 128] = outer[
                    dd * 32 : (dd + 1) * 32, g * 128 : (g + 1) * 128
                ]
    mean = dot(AB[...], WB[...]) * inverse_count
    mean = jnp.concatenate(
        [
            mean[(i // 4) * 32 : (i // 4 + 1) * 32, (i % 4) * 128 : (i % 4 + 1) * 128]
            for i in range(ROW)
        ],
        axis=0,
    )
    fetch(1).wait()
    fetch(6).wait()
    pair_mid = (pair_ref[...].reshape(ROW * TOK, 128).astype(F32) + mean).astype(BF16)
    MID[...] = pair_mid
    pair_norm = normalized(pair_mid.astype(F32))
    PNB[...] = pair_norm.astype(BF16)
    score_w = jnp.concatenate(
        [jnp.broadcast_to(smt_ref[h : h + 1, :], (ROW, 128)) for h in range(HEADS)], axis=0
    )
    every = dot_nt(pair_norm, score_w, lax.Precision.HIGHEST)
    lane_i = iota((TOK, 128), 1) % ROW
    scores = jnp.zeros((TOK, 128), F32)
    for i in range(ROW):
        scores = jnp.where(lane_i == i, every[i * TOK : (i + 1) * TOK], scores)
    shift = jnp.max(scores, axis=0, keepdims=True).astype(BF16).astype(F32)
    EY[0:TOK, :] = jnp.exp(scores - shift).astype(BF16)
    EY[TOK : TOK + 16, :] = jnp.broadcast_to(shift, (16, 128)).astype(BF16)

    def ez(to):
        return remote(
            EY, EX.at[x % 2, col], ez_s.at[to], ez_r.at[col], y=to, z=y, k=x // 2
        )

    def e_here(to):
        return jnp.logical_and(jnp.logical_and(to == y, z == y), owner)

    def ex(block, t):
        part = pl.ds(block * K, K)
        return remote(
            EX.at[x % 2, part],
            EX.at[x % 2, part],
            ex_s.at[block, t],
            ex_r.at[x % 2, block],
            x=lax.rem(x + t, X),
        )

    for to in range(Y):

        @pl.when(jnp.logical_not(e_here(to)))
        def _():
            ez(to).start()

        @pl.when(e_here(to))
        def _():
            EX[x % 2, col] = EY[...]

    hk(z).start()
    for t in near_first:
        block = lax.rem(z + t, Z)
        h_arrived(block * K + k)
        hk(block).start()
    fetch(10).wait()
    fetch(11).wait()
    for part in range(4):
        rows = slice(part * 128, (part + 1) * 128)
        pre = dot(PNB[rows, :], ti_ref[...])
        gate = pre[:, :512]
        hidden = (gate / (1.0 + jnp.exp(-gate)) * pre[:, 512:]).astype(BF16)
        out = (MID[rows, :].astype(F32) + dot(hidden, to_ref[...])).astype(BF16)
        pout_ref[part * 4 : (part + 1) * 4] = out.reshape(4, TOK, 128)

    @pl.when(owner)
    def _():
        for block in range(Z):
            for j in range(K):
                c = block * K + j

                @pl.when(jnp.logical_or(c != col, y != z))
                def _():
                    remote(EY, EX.at[x % 2, c], ez_s.at[0], ez_r.at[c], z=z).wait_recv()

            for t in (2, 1, 3):
                ex(block, t).start()

    for i in (7, 8, 9):
        fetch(i).wait()
    for t in range(Z):
        h_arrived(t * K + 1 - k)
    zeros = jnp.zeros((64, 256), BF16)
    for side in range(2):
        pay = jnp.concatenate(
            [pay_ref[...], zeros] if side == 0 else [zeros, pay_ref[...]], axis=0
        )
        for s in range(4):
            rows = HB[:, s * TOK : (s + 1) * TOK, :].reshape(NT, 128)
            VB[side * 4 + s] = dot(rows, pay).astype(BF16)
    gate = jax.nn.sigmoid(dot(NB[...], sw_ref[...]))

    weights = []
    for h in range(2):

        @pl.when(x != 2 * k + h)
        def _():
            for block in range(Z):
                part = pl.ds(block * K, K)
                remote(
                    EX.at[h, part], EX.at[h, part], ex_s.at[0, 0], ex_r.at[h, block], x=x
                ).wait_recv()

        shifts = EX[h, :, TOK : TOK + 16, :].astype(F32)[:, 0:1, :]
        factor = jnp.exp(shifts - jnp.max(shifts, axis=0, keepdims=True))
        w = EX[h, :, 0:TOK, :].astype(F32) * factor
        total = jnp.sum(jnp.sum(w, axis=0, keepdims=True), axis=1, keepdims=True)
        weights.append(jnp.transpose((w / total).reshape(NT, 128)).astype(BF16))
    weights = jnp.concatenate(weights, axis=0)
    head = iota((ROW, 256), 1) // 32
    averages = []
    for s in range(SEQ):
        full = dot(weights, VB[s])
        for half in range(2):
            average = jnp.zeros((ROW, 256), F32)
            for g in range(HEADS):
                start = half * 128 + g * ROW
                average = jnp.where(head == g, full[start : start + ROW], average)
            averages.append(average)
    gated = (gate * jnp.concatenate(averages, axis=0)).astype(BF16)
    out = h_ref[...].reshape(SEQ * TOK, 64).astype(F32) + dot_nt(gated, rett_ref[...])
    align_ref[...] = out.astype(BF16).reshape(SEQ, TOK, 64)

    for t in range(1, Y):
        right_y(t).wait_send()
    for block in range(Y):
        for t in range(1, X):
            right_x(block, t).wait_send()

        @pl.when(jnp.logical_not(e_here(block)))
        def _():
            ez(block).wait_send()

    for t in range(1, Z):
        left_z(t).wait_send()
        hz(t).wait_send()
    for block in range(Z):
        hk(block).wait_send()
        for h in range(2):

            @pl.when(jnp.logical_not(left_here(block, h)))
            def _():
                left_x(block, h).wait_send()

    @pl.when(owner)
    def _():
        for block in range(Y):
            left_k(block).wait_send()
        for block in range(Z):
            for t in range(1, X):
                ex(block, t).wait_send()


def body(h, pair, seq, tok, pp, mm, sm, pay, sw, ret, ti, to, *, Y, Z):
    R, C = Y * X, Z * K
    NT = C * TOK
    dma = pltpu.SemaphoreType.DMA
    args = (h, pair, seq.reshape(1, -1), tok.reshape(1, -1), pp, mm)
    args += (sm.T, pay, sw, ret.T, ti, to)
    return pl.pallas_call(
        functools.partial(kernel, Y, Z),
        out_shape=(
            pltpu.VMEM(h.shape, BF16),
            pltpu.VMEM(pair.shape, BF16),
        ),
        in_specs=[pl.BlockSpec(memory_space=pl.ANY)] * 12,
        out_specs=(pl.BlockSpec(memory_space=pltpu.VMEM),) * 2,
        scratch_shapes=[pltpu.VMEM(v.shape, v.dtype) for v in args]
        + [
            pltpu.VMEM((R, 16, 512), BF16),
            pltpu.VMEM((Z, 2, 16, 256), BF16),
            pltpu.VMEM((R, 16, 256), BF16),
            pltpu.VMEM((C, 128, 128), BF16),
            pltpu.VMEM((TOK + 16, 128), BF16),
            pltpu.VMEM((2, C, TOK + 16, 128), BF16),
            pltpu.VMEM((1024, 128), F32),
            pltpu.VMEM((4096, 512), BF16),
            pltpu.VMEM((128, 4096), BF16),
            pltpu.VMEM((1024, R * SEQ), BF16),
            pltpu.VMEM((SEQ, NT, 256), BF16),
            pltpu.VMEM((256, 64), BF16),
            pltpu.VMEM((512, 128), BF16),
            pltpu.VMEM((512, 128), BF16),
            dma((12,)),
            dma((Y,)),
            dma((Y, X)),
            dma((R,)),
            dma((Z,)),
            dma((Z,)),
            dma((Z, 2)),
            dma((R,)),
            dma((Y,)),
            dma((Y,)),
            dma((Z,)),
            dma((Z,)),
            dma((C,)),
            dma((Y,)),
            dma((C,)),
            dma((Z, X)),
            dma((2, Z)),
        ],
        compiler_params=pltpu.CompilerParams(
            collective_id=0, has_side_effects=True, vmem_limit_bytes=60 * 1024 * 1024
        ),
        cost_estimate=pl.CostEstimate(
            flops=3_000_000_000, bytes_accessed=2_000_000, transcendentals=400_000
        ),
    )(*args)


def solution(mesh):
    Y, Z = mesh.shape["row"] // X, mesh.shape["col"] // K
    split = Mesh(mesh.devices.reshape(Y, X, Z, K), ("y", "x", "z", "k"))
    tiled = P(("y", "x"), ("z", "k"), None)
    return jax.shard_map(
        functools.partial(body, Y=Y, Z=Z),
        mesh=split,
        in_specs=(tiled, tiled) + (P(),) * 10,
        out_specs=(tiled, tiled),
        check_vma=False,
    )
```

```python
import functools

import jax
import jax.numpy as jnp
from jax import lax
from jax.experimental import pallas as pl
from jax.experimental.pallas import tpu as pltpu
from jax.sharding import Mesh
from jax.sharding import PartitionSpec as P

F32 = jnp.float32
BF16 = jnp.bfloat16
MESH = pl.DeviceIdType.MESH
epsilon = 1e-05

X, K = 4, 2
SEQ = 8
TOK = 32
ROW = 16
HEADS = 8


def iota(shape, dim):
    return lax.broadcasted_iota(jnp.int32, shape, dim)


def one_hot(condition):
    return jnp.where(condition, 1.0, 0.0).astype(BF16)


def dot(a, b):
    return jnp.dot(a, b, preferred_element_type=F32)


def dot_nt(a, b, precision=None):
    return lax.dot_general(
        a, b, (((1,), (1,)), ((), ())), precision=precision, preferred_element_type=F32
    )


def normalized(source):
    center = source - jnp.mean(source, axis=-1, keepdims=True)
    spread = jnp.mean(center * center, axis=-1, keepdims=True)
    return center * lax.rsqrt(spread + epsilon)


def kernel(Y, Z, *refs):
    R = Y * X
    C = Z * K
    NS = R * SEQ
    NT = C * TOK
    hbm, (align_ref, pout_ref), refs = refs[:12], refs[12:14], refs[14:]
    local, refs = refs[:12], refs[12:]
    h_ref, pair_ref, seq_ref, tok_ref, pp_ref, mm_ref = local[:6]
    smt_ref, pay_ref, sw_ref, rett_ref, ti_ref, to_ref = local[6:]
    RB, LZ, LB, HB, EY, EX, MF, WB, AB, RT, VB, NB, MID, PNB, GA, GB = refs[:16]
    in_s, ry_s, rx_s, r_r, lz_s, lz_r, lx_s, l_r, lk_s, lk_r = refs[16:26]
    hz_s, hk_s, h_r, ez_s, ez_r, ex_s, ex_r = refs[26:]
    y, x = lax.axis_index("y"), lax.axis_index("x")
    z, k = lax.axis_index("z"), lax.axis_index("k")
    row = y * X + x
    col = z * K + k
    owner = k == x // 2
    far_first = sorted(range(1, Z), key=lambda t: -min(t, Z - t))
    near_first = far_first[::-1]

    def remote(src, dst, send, recv, **to):
        return pltpu.make_async_remote_copy(
            src_ref=src,
            dst_ref=dst,
            send_sem=send,
            recv_sem=recv,
            device_id=to,
            device_id_type=MESH,
        )

    barrier = pltpu.get_barrier_semaphore()
    for axis, at, size in (("y", y, Y), ("z", z, Z), ("x", x, X), ("k", k, K)):
        for t in range(1, size):
            pl.semaphore_signal(
                barrier, inc=1, device_id={axis: lax.rem(at + t, size)}, device_id_type=MESH
            )

    def fetch(i):
        return pltpu.make_async_copy(hbm[i], local[i], in_s.at[i])

    for i in (0, 4, 3, 2, 5, 1, 6, 10, 11, 7, 8, 9):
        fetch(i).start()
    for i in (0, 4, 3, 2):
        fetch(i).wait()

    hf = h_ref[...].reshape(SEQ * TOK, 64).astype(F32)
    norm_f = normalized(hf)
    NB[...] = norm_f.astype(BF16)
    tokens = tok_ref[...].astype(F32)
    seqs = seq_ref[...].astype(F32)
    hit = iota((TOK, NT), 1) == col * TOK + iota((TOK, NT), 0)
    live_tok = jnp.sum(jnp.where(hit, tokens, 0.0), axis=1, keepdims=True)
    live_tok = jnp.concatenate([live_tok] * SEQ, axis=0)
    hit = iota((SEQ * TOK, NS), 1) == row * SEQ + iota((SEQ * TOK, NS), 0) // TOK
    live_seq = jnp.sum(jnp.where(hit, seqs, 0.0), axis=1, keepdims=True)
    inverse_count = 1.0 / jnp.maximum(jnp.sum(seqs, axis=1, keepdims=True), 1.0)
    norm = (norm_f * live_tok).astype(BF16)

    pp = pp_ref[...]
    mine = iota((256, 128), 0) % 4 == iota((256, 128), 1) // 32
    a, b = iota((64, 256), 0), iota((64, 256), 1)
    left_w = dot(pp, one_hot(iota((64, 128), 0) == iota((64, 128), 1) % 32)).astype(BF16)
    spread = dot(norm, left_w) * live_seq
    spread = jnp.where(mine, spread, 0.0).astype(BF16)
    pick = one_hot(
        (a % 8 == b // 32) & ((b % 32) // 4 == 4 * (a // 32) + 2 * ((a // 8) % 2) + (a // 16) % 2)
    )
    packed = dot(pick, spread).astype(BF16)
    for h in range(2):
        for t in range(2):
            LZ[z, h, :, t * 128 : (t + 1) * 128] = packed[(h * 2 + t) * 16 : (h * 2 + t + 1) * 16]

    right_t = dot_nt(one_hot(iota((32, 64), 1) == 32 + iota((32, 64), 0)), pp).astype(BF16)
    spread = []
    for s in range(SEQ):
        one = norm[s * TOK : (s + 1) * TOK]
        spread.append(dot_nt(right_t, jnp.concatenate([one] * 4, axis=0)))
    spread = jnp.concatenate(spread, axis=0)
    spread = jnp.where(mine, spread, 0.0).astype(BF16)
    pick = one_hot((a % 8 == b // 32) & ((b % 32) // 4 == ((a // 8) % 2) * 4 + a // 16))
    packed = dot(pick, spread).astype(BF16)
    for t in range(4):
        RB[row, :, t * 128 : (t + 1) * 128] = packed[t * 16 : (t + 1) * 16]

    pl.semaphore_wait(barrier, (Y - 1) + (Z - 1) + (X - 1) + (K - 1))

    def left_z(t):
        return remote(LZ.at[z], LZ.at[z], lz_s.at[t], lz_r.at[z], z=lax.rem(z + t, Z))

    def left_x(block, h):
        return remote(
            LZ.at[block, h],
            LB.at[row],
            lx_s.at[block, h],
            l_r.at[row],
            y=block,
            x=2 * k + h,
        )

    def left_here(block, h):
        return jnp.logical_and(block == y, 2 * k + h == x)

    def left_forward(block):
        for h in range(2):

            @pl.when(jnp.logical_not(left_here(block, h)))
            def _():
                left_x(block, h).start()

            @pl.when(left_here(block, h))
            def _():
                LB[row] = LZ[block, h]

    def left_k(block):
        part = pl.ds(block * X, X)
        return remote(LB.at[part], LB.at[part], lk_s.at[block], lk_r.at[block], k=1 - k)

    def right_y(t):
        return remote(RB.at[row], RB.at[row], ry_s.at[t], r_r.at[row], y=lax.rem(y + t, Y))

    def right_x(block, t):
        r = block * X + x
        return remote(
            RB.at[r], RB.at[r], rx_s.at[block, t], r_r.at[r], x=lax.rem(x + t, X)
        )

    def right_arrived(r):
        remote(RB.at[r], RB.at[r], ry_s.at[0], r_r.at[r], x=x).wait_recv()

    for t in far_first:
        left_z(t).start()
    for t in far_first:
        right_y(t).start()
    for t in (2, 1, 3):
        right_x(y, t).start()

    u, v = iota((64, 128), 0), iota((64, 128), 1)
    HB[col] = (
        dot(norm[:128], one_hot(u == v)) + dot(norm[128:], one_hot(u + 64 == v))
    ).astype(BF16)

    fetch(5).wait()
    MF[...] = mm_ref[...].astype(F32)
    WB[...] = jnp.zeros_like(WB)
    for d in range(32):
        part = MF[pl.ds(d, 32, stride=32), :].astype(BF16)
        for i in range(4):
            WB[d * 128 + i * 32 : d * 128 + (i + 1) * 32, i * 128 : (i + 1) * 128] = part

    half = Y // 2
    outer = jnp.logical_or(z < Y // 4, z >= Y - Y // 4)

    def right_forward(block):
        @pl.when(block != y)
        def _():
            right_arrived(block * X + x)
            for t in (2, 1, 3):
                right_x(block, t).start()

    def left_next(block):
        @pl.when(block != z)
        def _():
            remote(
                LZ.at[block], LZ.at[block], lz_s.at[0], lz_r.at[block], z=z
            ).wait_recv()

        left_forward(block)

    for i in range(half):
        right_forward(i)
    for i in range(half):
        left_next(jnp.where(outer, i, half - 1 - i))
    def hz(t):
        return remote(HB.at[col], HB.at[col], hz_s.at[t], h_r.at[col], z=lax.rem(z + t, Z))

    def hk(block):
        c = block * K + k
        return remote(HB.at[c], HB.at[c], hk_s.at[block], h_r.at[c], k=1 - k)

    def h_arrived(c):
        remote(HB.at[c], HB.at[c], hz_s.at[0], h_r.at[c], z=z).wait_recv()

    for t in far_first:
        hz(t).start()
    for i in range(half, Y):
        block = jnp.where(outer, Y + half - 1 - i, i)
        right_forward(block)
        left_next(block)

    @pl.when(owner)
    def _():
        for block in range(Y):
            for other in range(X):
                r = block * X + other

                @pl.when(r != row)
                def _():
                    remote(LB.at[r], LB.at[r], lx_s.at[0, 0], l_r.at[r], x=x).wait_recv()

            left_k(block).start()

    for block in range(Y):
        for t in range(1, X):
            right_arrived(block * X + lax.rem(x + t, X))
    for half in range(2):
        right = RB[...].astype(F32).reshape(R, 2, SEQ, 512)[:, half].reshape(NS, 512)
        RT[half * 512 : (half + 1) * 512, :] = jnp.transpose(right).astype(BF16)

    @pl.when(jnp.logical_not(owner))
    def _():
        for block in range(Y):
            part = pl.ds(block * X, X)
            remote(LB.at[part], LB.at[part], lk_s.at[0], lk_r.at[block], y=y).wait_recv()

    left = LB[...].astype(F32).reshape(R, 2, SEQ, 256)
    left = jnp.concatenate(
        [left[:, 0].reshape(NS, 256), left[:, 1].reshape(NS, 256)], axis=1
    ).astype(BF16)
    for part in range(4):
        outer = dot(RT[part * 256 : (part + 1) * 256, :], left).astype(BF16)
        for dd in range(8):
            d = part * 8 + dd
            for g in range(4):
                AB[g * 32 : (g + 1) * 32, d * 128 : (d + 1) * 128] = outer[
                    dd * 32 : (dd + 1) * 32, g * 128 : (g + 1) * 128
                ]
    mean = dot(AB[...], WB[...]) * inverse_count
    mean = jnp.concatenate(
        [
            mean[(i // 4) * 32 : (i // 4 + 1) * 32, (i % 4) * 128 : (i % 4 + 1) * 128]
            for i in range(ROW)
        ],
        axis=0,
    )
    fetch(1).wait()
    fetch(6).wait()
    pair_mid = (pair_ref[...].reshape(ROW * TOK, 128).astype(F32) + mean).astype(BF16)
    MID[...] = pair_mid
    pair_norm = normalized(pair_mid.astype(F32))
    PNB[...] = pair_norm.astype(BF16)
    score_w = jnp.concatenate(
        [jnp.broadcast_to(smt_ref[h : h + 1, :], (ROW, 128)) for h in range(HEADS)], axis=0
    )
    every = dot_nt(pair_norm, score_w, lax.Precision.HIGHEST)
    lane_i = iota((TOK, 128), 1) % ROW
    scores = jnp.zeros((TOK, 128), F32)
    for i in range(ROW):
        scores = jnp.where(lane_i == i, every[i * TOK : (i + 1) * TOK], scores)
    shift = jnp.max(scores, axis=0, keepdims=True).astype(BF16).astype(F32)
    EY[0:TOK, :] = jnp.exp(scores - shift).astype(BF16)
    EY[TOK : TOK + 16, :] = jnp.broadcast_to(shift, (16, 128)).astype(BF16)

    def ez(to):
        return remote(
            EY, EX.at[x % 2, col], ez_s.at[to], ez_r.at[col], y=to, z=y, k=x // 2
        )

    def e_here(to):
        return jnp.logical_and(jnp.logical_and(to == y, z == y), owner)

    def ex(block, t):
        part = pl.ds(block * K, K)
        return remote(
            EX.at[x % 2, part],
            EX.at[x % 2, part],
            ex_s.at[block, t],
            ex_r.at[x % 2, block],
            x=lax.rem(x + t, X),
        )

    for to in range(Y):

        @pl.when(jnp.logical_not(e_here(to)))
        def _():
            ez(to).start()

        @pl.when(e_here(to))
        def _():
            EX[x % 2, col] = EY[...]

    hk(z).start()
    for t in near_first:
        block = lax.rem(z + t, Z)
        h_arrived(block * K + k)
        hk(block).start()
    fetch(10).wait()
    fetch(11).wait()
    for part in range(4):
        rows = slice(part * 128, (part + 1) * 128)
        pre = dot(PNB[rows, :], ti_ref[...])
        gate = pre[:, :512]
        hidden = (gate / (1.0 + jnp.exp(-gate)) * pre[:, 512:]).astype(BF16)
        out = (MID[rows, :].astype(F32) + dot(hidden, to_ref[...])).astype(BF16)
        pout_ref[part * 4 : (part + 1) * 4] = out.reshape(4, TOK, 128)

    @pl.when(owner)
    def _():
        for block in range(Z):
            for j in range(K):
                c = block * K + j

                @pl.when(jnp.logical_or(c != col, y != z))
                def _():
                    remote(EY, EX.at[x % 2, c], ez_s.at[0], ez_r.at[c], z=z).wait_recv()

            for t in (2, 1, 3):
                ex(block, t).start()

    for i in (7, 8, 9):
        fetch(i).wait()
    for t in range(Z):
        h_arrived(t * K + 1 - k)
    zeros = jnp.zeros((64, 256), BF16)
    for side in range(2):
        pay = jnp.concatenate(
            [pay_ref[...], zeros] if side == 0 else [zeros, pay_ref[...]], axis=0
        )
        for s in range(4):
            rows = HB[:, s * TOK : (s + 1) * TOK, :].reshape(NT, 128)
            VB[side * 4 + s] = dot(rows, pay).astype(BF16)
    GA[...] = jax.nn.sigmoid(dot(NB[...], sw_ref[...])).reshape(SEQ, 2, ROW, 256)

    head = iota((ROW, 256), 1) // 32
    for i in range(2):
        h = lax.rem(x + i, 2)

        @pl.when(x != 2 * k + h)
        def _():
            for block in range(Z):
                part = pl.ds(block * K, K)
                remote(
                    EX.at[h, part], EX.at[h, part], ex_s.at[0, 0], ex_r.at[h, block], x=x
                ).wait_recv()

        shifts = EX[h, :, TOK : TOK + 16, :].astype(F32)[:, 0:1, :]
        factor = jnp.exp(shifts - jnp.max(shifts, axis=0, keepdims=True))
        w = EX[h, :, 0:TOK, :].astype(F32) * factor
        total = jnp.sum(jnp.sum(w, axis=0, keepdims=True), axis=1, keepdims=True)
        weights = jnp.transpose((w / total).reshape(NT, 128)).astype(BF16)
        for s in range(SEQ):
            full = dot(weights, VB[s])
            average = jnp.zeros((ROW, 256), F32)
            for g in range(HEADS):
                average = jnp.where(head == g, full[g * ROW : (g + 1) * ROW], average)
            GB[s, h] = (GA[s, h] * average).astype(BF16)
    gated = GB[...].reshape(SEQ * TOK, 256)
    out = h_ref[...].reshape(SEQ * TOK, 64).astype(F32) + dot_nt(gated, rett_ref[...])
    align_ref[...] = out.astype(BF16).reshape(SEQ, TOK, 64)

    for t in range(1, Y):
        right_y(t).wait_send()
    for block in range(Y):
        for t in range(1, X):
            right_x(block, t).wait_send()

        @pl.when(jnp.logical_not(e_here(block)))
        def _():
            ez(block).wait_send()

    for t in range(1, Z):
        left_z(t).wait_send()
        hz(t).wait_send()
    for block in range(Z):
        hk(block).wait_send()
        for h in range(2):

            @pl.when(jnp.logical_not(left_here(block, h)))
            def _():
                left_x(block, h).wait_send()

    @pl.when(owner)
    def _():
        for block in range(Y):
            left_k(block).wait_send()
        for block in range(Z):
            for t in range(1, X):
                ex(block, t).wait_send()


def body(h, pair, seq, tok, pp, mm, sm, pay, sw, ret, ti, to, *, Y, Z):
    R, C = Y * X, Z * K
    NT = C * TOK
    dma = pltpu.SemaphoreType.DMA
    args = (h, pair, seq.reshape(1, -1), tok.reshape(1, -1), pp, mm)
    args += (sm.T, pay, sw, ret.T, ti, to)
    return pl.pallas_call(
        functools.partial(kernel, Y, Z),
        out_shape=(
            pltpu.VMEM(h.shape, BF16),
            pltpu.VMEM(pair.shape, BF16),
        ),
        in_specs=[pl.BlockSpec(memory_space=pl.ANY)] * 12,
        out_specs=(pl.BlockSpec(memory_space=pltpu.VMEM),) * 2,
        scratch_shapes=[pltpu.VMEM(v.shape, v.dtype) for v in args]
        + [
            pltpu.VMEM((R, 16, 512), BF16),
            pltpu.VMEM((Z, 2, 16, 256), BF16),
            pltpu.VMEM((R, 16, 256), BF16),
            pltpu.VMEM((C, 128, 128), BF16),
            pltpu.VMEM((TOK + 16, 128), BF16),
            pltpu.VMEM((2, C, TOK + 16, 128), BF16),
            pltpu.VMEM((1024, 128), F32),
            pltpu.VMEM((4096, 512), BF16),
            pltpu.VMEM((128, 4096), BF16),
            pltpu.VMEM((1024, R * SEQ), BF16),
            pltpu.VMEM((SEQ, NT, 256), BF16),
            pltpu.VMEM((256, 64), BF16),
            pltpu.VMEM((512, 128), BF16),
            pltpu.VMEM((512, 128), BF16),
            pltpu.VMEM((SEQ, 2, ROW, 256), F32),
            pltpu.VMEM((SEQ, 2, ROW, 256), BF16),
            dma((12,)),
            dma((Y,)),
            dma((Y, X)),
            dma((R,)),
            dma((Z,)),
            dma((Z,)),
            dma((Z, 2)),
            dma((R,)),
            dma((Y,)),
            dma((Y,)),
            dma((Z,)),
            dma((Z,)),
            dma((C,)),
            dma((Y,)),
            dma((C,)),
            dma((Z, X)),
            dma((2, Z)),
        ],
        compiler_params=pltpu.CompilerParams(
            collective_id=0, has_side_effects=True, vmem_limit_bytes=60 * 1024 * 1024
        ),
        cost_estimate=pl.CostEstimate(
            flops=3_000_000_000, bytes_accessed=2_000_000, transcendentals=400_000
        ),
    )(*args)


def solution(mesh):
    Y, Z = mesh.shape["row"] // X, mesh.shape["col"] // K
    split = Mesh(mesh.devices.reshape(Y, X, Z, K), ("y", "x", "z", "k"))
    tiled = P(("y", "x"), ("z", "k"), None)
    return jax.shard_map(
        functools.partial(body, Y=Y, Z=Z),
        mesh=split,
        in_specs=(tiled, tiled) + (P(),) * 10,
        out_specs=(tiled, tiled),
        check_vma=False,
    )
```

```python
import functools

import jax
import jax.numpy as jnp
from jax import lax
from jax.experimental import pallas as pl
from jax.experimental.pallas import tpu as pltpu
from jax.sharding import Mesh
from jax.sharding import PartitionSpec as P

F32 = jnp.float32
BF16 = jnp.bfloat16
MESH = pl.DeviceIdType.MESH
epsilon = 1e-05

X, K = 4, 2
SEQ = 8
TOK = 32
ROW = 16
HEADS = 8


def iota(shape, dim):
    return lax.broadcasted_iota(jnp.int32, shape, dim)


def one_hot(condition):
    return jnp.where(condition, 1.0, 0.0).astype(BF16)


def dot(a, b):
    return jnp.dot(a, b, preferred_element_type=F32)


def dot_nt(a, b, precision=None):
    return lax.dot_general(
        a, b, (((1,), (1,)), ((), ())), precision=precision, preferred_element_type=F32
    )


def normalized(source):
    center = source - jnp.mean(source, axis=-1, keepdims=True)
    spread = jnp.mean(center * center, axis=-1, keepdims=True)
    return center * lax.rsqrt(spread + epsilon)


def kernel(Y, Z, *refs):
    R = Y * X
    C = Z * K
    NS = R * SEQ
    NT = C * TOK
    hbm, (align_ref, pout_ref), refs = refs[:12], refs[12:14], refs[14:]
    local, refs = refs[:12], refs[12:]
    h_ref, pair_ref, seq_ref, tok_ref, pp_ref, mm_ref = local[:6]
    smt_ref, pay_ref, sw_ref, rett_ref, ti_ref, to_ref = local[6:]
    RB, LZ, LB, HB, EY, EX, MF, WB, AB, RT, VB, NB, MID, PNB, GA, GB = refs[:16]
    in_s, ry_s, rx_s, r_r, lz_s, lz_r, lx_s, l_r, lk_s, lk_r = refs[16:26]
    hz_s, hk_s, h_r, ez_s, ez_r, ex_s, ex_r = refs[26:]
    y, x = lax.axis_index("y"), lax.axis_index("x")
    z, k = lax.axis_index("z"), lax.axis_index("k")
    row = y * X + x
    col = z * K + k
    owner = k == x // 2
    far_first = sorted(range(1, Z), key=lambda t: -min(t, Z - t))
    near_first = far_first[::-1]

    def remote(src, dst, send, recv, **to):
        return pltpu.make_async_remote_copy(
            src_ref=src,
            dst_ref=dst,
            send_sem=send,
            recv_sem=recv,
            device_id=to,
            device_id_type=MESH,
        )

    def fetch(i):
        return pltpu.make_async_copy(hbm[i], local[i], in_s.at[i])

    for i in (0, 4, 3, 2):
        fetch(i).start()

    barrier = pltpu.get_barrier_semaphore()
    steps = [(axis, t) for axis, n in (("y", Y), ("z", Z), ("x", X), ("k", K)) for t in range(1, n)]
    size, place = {"y": Y, "z": Z, "x": X, "k": K}, {"y": y, "z": z, "x": x, "k": k}
    for axis, t in sorted(steps, key=lambda step: -min(step[1], size[step[0]] - step[1])):
        pl.semaphore_signal(
            barrier,
            inc=1,
            device_id={axis: lax.rem(place[axis] + t, size[axis])},
            device_id_type=MESH,
        )

    for i in (5, 1, 6, 10, 11, 7, 8, 9):
        fetch(i).start()
    for i in (0, 4, 3, 2):
        fetch(i).wait()

    hf = h_ref[...].reshape(SEQ * TOK, 64).astype(F32)
    norm_f = normalized(hf)
    NB[...] = norm_f.astype(BF16)
    tokens = tok_ref[...].astype(F32)
    seqs = seq_ref[...].astype(F32)
    hit = iota((TOK, NT), 1) == col * TOK + iota((TOK, NT), 0)
    live_tok = jnp.sum(jnp.where(hit, tokens, 0.0), axis=1, keepdims=True)
    live_tok = jnp.concatenate([live_tok] * SEQ, axis=0)
    hit = iota((SEQ * TOK, NS), 1) == row * SEQ + iota((SEQ * TOK, NS), 0) // TOK
    live_seq = jnp.sum(jnp.where(hit, seqs, 0.0), axis=1, keepdims=True)
    inverse_count = 1.0 / jnp.maximum(jnp.sum(seqs, axis=1, keepdims=True), 1.0)
    norm = (norm_f * live_tok).astype(BF16)

    pp = pp_ref[...]
    mine = iota((256, 128), 0) % 4 == iota((256, 128), 1) // 32
    a, b = iota((64, 256), 0), iota((64, 256), 1)
    left_w = dot(pp, one_hot(iota((64, 128), 0) == iota((64, 128), 1) % 32)).astype(BF16)
    spread = dot(norm, left_w) * live_seq
    spread = jnp.where(mine, spread, 0.0).astype(BF16)
    pick = one_hot(
        (a % 8 == b // 32) & ((b % 32) // 4 == 4 * (a // 32) + 2 * ((a // 8) % 2) + (a // 16) % 2)
    )
    packed = dot(pick, spread).astype(BF16)
    for h in range(2):
        for t in range(2):
            LZ[z, h, :, t * 128 : (t + 1) * 128] = packed[(h * 2 + t) * 16 : (h * 2 + t + 1) * 16]

    right_t = dot_nt(one_hot(iota((32, 64), 1) == 32 + iota((32, 64), 0)), pp).astype(BF16)
    spread = []
    for s in range(SEQ):
        one = norm[s * TOK : (s + 1) * TOK]
        spread.append(dot_nt(right_t, jnp.concatenate([one] * 4, axis=0)))
    spread = jnp.concatenate(spread, axis=0)
    spread = jnp.where(mine, spread, 0.0).astype(BF16)
    pick = one_hot((a % 8 == b // 32) & ((b % 32) // 4 == ((a // 8) % 2) * 4 + a // 16))
    packed = dot(pick, spread).astype(BF16)
    for t in range(4):
        RB[row, :, t * 128 : (t + 1) * 128] = packed[t * 16 : (t + 1) * 16]

    pl.semaphore_wait(barrier, (Y - 1) + (Z - 1) + (X - 1) + (K - 1))

    def left_z(t):
        return remote(LZ.at[z], LZ.at[z], lz_s.at[t], lz_r.at[z], z=lax.rem(z + t, Z))

    def left_x(block, h):
        return remote(
            LZ.at[block, h],
            LB.at[row],
            lx_s.at[block, h],
            l_r.at[row],
            y=block,
            x=2 * k + h,
        )

    def left_here(block, h):
        return jnp.logical_and(block == y, 2 * k + h == x)

    def left_forward(block):
        for h in range(2):

            @pl.when(jnp.logical_not(left_here(block, h)))
            def _():
                left_x(block, h).start()

            @pl.when(left_here(block, h))
            def _():
                LB[row] = LZ[block, h]

    def left_k(block):
        part = pl.ds(block * X, X)
        return remote(LB.at[part], LB.at[part], lk_s.at[block], lk_r.at[block], k=1 - k)

    def right_y(t):
        return remote(RB.at[row], RB.at[row], ry_s.at[t], r_r.at[row], y=lax.rem(y + t, Y))

    def right_x(block, t):
        r = block * X + x
        return remote(
            RB.at[r], RB.at[r], rx_s.at[block, t], r_r.at[r], x=lax.rem(x + t, X)
        )

    def right_arrived(r):
        remote(RB.at[r], RB.at[r], ry_s.at[0], r_r.at[r], x=x).wait_recv()

    for t in far_first:
        left_z(t).start()
    for t in far_first:
        right_y(t).start()
    for t in (2, 1, 3):
        right_x(y, t).start()

    u, v = iota((64, 128), 0), iota((64, 128), 1)
    HB[col] = (
        dot(norm[:128], one_hot(u == v)) + dot(norm[128:], one_hot(u + 64 == v))
    ).astype(BF16)

    fetch(5).wait()
    MF[...] = mm_ref[...].astype(F32)
    WB[...] = jnp.zeros_like(WB)
    for d in range(32):
        part = MF[pl.ds(d, 32, stride=32), :].astype(BF16)
        for i in range(4):
            WB[d * 128 + i * 32 : d * 128 + (i + 1) * 32, i * 128 : (i + 1) * 128] = part

    half = Y // 2
    outer = jnp.logical_or(z < Y // 4, z >= Y - Y // 4)

    def right_forward(block):
        @pl.when(block != y)
        def _():
            right_arrived(block * X + x)
            for t in (2, 1, 3):
                right_x(block, t).start()

    def left_next(block):
        @pl.when(block != z)
        def _():
            remote(
                LZ.at[block], LZ.at[block], lz_s.at[0], lz_r.at[block], z=z
            ).wait_recv()

        left_forward(block)

    for i in range(half):
        right_forward(i)
    for i in range(half):
        left_next(jnp.where(outer, i, half - 1 - i))
    def hz(t):
        return remote(HB.at[col], HB.at[col], hz_s.at[t], h_r.at[col], z=lax.rem(z + t, Z))

    def hk(block):
        c = block * K + k
        return remote(HB.at[c], HB.at[c], hk_s.at[block], h_r.at[c], k=1 - k)

    def h_arrived(c):
        remote(HB.at[c], HB.at[c], hz_s.at[0], h_r.at[c], z=z).wait_recv()

    for t in far_first:
        hz(t).start()
    for i in range(half, Y):
        block = jnp.where(outer, Y + half - 1 - i, i)
        right_forward(block)
        left_next(block)

    @pl.when(owner)
    def _():
        for block in range(Y):
            for other in range(X):
                r = block * X + other

                @pl.when(r != row)
                def _():
                    remote(LB.at[r], LB.at[r], lx_s.at[0, 0], l_r.at[r], x=x).wait_recv()

            left_k(block).start()

    for block in range(Y):
        for t in range(1, X):
            right_arrived(block * X + lax.rem(x + t, X))
    for half in range(2):
        right = RB[...].astype(F32).reshape(R, 2, SEQ, 512)[:, half].reshape(NS, 512)
        RT[half * 512 : (half + 1) * 512, :] = jnp.transpose(right).astype(BF16)

    @pl.when(jnp.logical_not(owner))
    def _():
        for block in range(Y):
            part = pl.ds(block * X, X)
            remote(LB.at[part], LB.at[part], lk_s.at[0], lk_r.at[block], y=y).wait_recv()

    left = LB[...].astype(F32).reshape(R, 2, SEQ, 256)
    left = jnp.concatenate(
        [left[:, 0].reshape(NS, 256), left[:, 1].reshape(NS, 256)], axis=1
    ).astype(BF16)
    for part in range(4):
        outer = dot(RT[part * 256 : (part + 1) * 256, :], left).astype(BF16)
        for dd in range(8):
            d = part * 8 + dd
            for g in range(4):
                AB[g * 32 : (g + 1) * 32, d * 128 : (d + 1) * 128] = outer[
                    dd * 32 : (dd + 1) * 32, g * 128 : (g + 1) * 128
                ]
    mean = dot(AB[...], WB[...]) * inverse_count
    mean = jnp.concatenate(
        [
            mean[(i // 4) * 32 : (i // 4 + 1) * 32, (i % 4) * 128 : (i % 4 + 1) * 128]
            for i in range(ROW)
        ],
        axis=0,
    )
    fetch(1).wait()
    fetch(6).wait()
    pair_mid = (pair_ref[...].reshape(ROW * TOK, 128).astype(F32) + mean).astype(BF16)
    MID[...] = pair_mid
    pair_norm = normalized(pair_mid.astype(F32))
    PNB[...] = pair_norm.astype(BF16)
    score_w = jnp.concatenate(
        [jnp.broadcast_to(smt_ref[h : h + 1, :], (ROW, 128)) for h in range(HEADS)], axis=0
    )
    every = dot_nt(pair_norm, score_w, lax.Precision.HIGHEST)
    lane_i = iota((TOK, 128), 1) % ROW
    scores = jnp.zeros((TOK, 128), F32)
    for i in range(ROW):
        scores = jnp.where(lane_i == i, every[i * TOK : (i + 1) * TOK], scores)
    shift = jnp.max(scores, axis=0, keepdims=True).astype(BF16).astype(F32)
    EY[0:TOK, :] = jnp.exp(scores - shift).astype(BF16)
    EY[TOK : TOK + 16, :] = jnp.broadcast_to(shift, (16, 128)).astype(BF16)

    def ez(to):
        return remote(
            EY, EX.at[x % 2, col], ez_s.at[to], ez_r.at[col], y=to, z=y, k=x // 2
        )

    def e_here(to):
        return jnp.logical_and(jnp.logical_and(to == y, z == y), owner)

    def ex(block, t):
        part = pl.ds(block * K, K)
        return remote(
            EX.at[x % 2, part],
            EX.at[x % 2, part],
            ex_s.at[block, t],
            ex_r.at[x % 2, block],
            x=lax.rem(x + t, X),
        )

    for to in range(Y):

        @pl.when(jnp.logical_not(e_here(to)))
        def _():
            ez(to).start()

        @pl.when(e_here(to))
        def _():
            EX[x % 2, col] = EY[...]

    hk(z).start()
    for t in near_first:
        block = lax.rem(z + t, Z)
        h_arrived(block * K + k)
        hk(block).start()
    fetch(10).wait()
    fetch(11).wait()
    for part in range(4):
        rows = slice(part * 128, (part + 1) * 128)
        pre = dot(PNB[rows, :], ti_ref[...])
        gate = pre[:, :512]
        hidden = (gate / (1.0 + jnp.exp(-gate)) * pre[:, 512:]).astype(BF16)
        out = (MID[rows, :].astype(F32) + dot(hidden, to_ref[...])).astype(BF16)
        pout_ref[part * 4 : (part + 1) * 4] = out.reshape(4, TOK, 128)

    for t in range(1, Y):
        right_y(t).wait_send()
    for block in range(Y):
        for t in range(1, X):
            right_x(block, t).wait_send()
    for t in range(1, Z):
        left_z(t).wait_send()
        hz(t).wait_send()
    for block in range(Z):
        hk(block).wait_send()
        for h in range(2):

            @pl.when(jnp.logical_not(left_here(block, h)))
            def _():
                left_x(block, h).wait_send()

    @pl.when(owner)
    def _():
        for block in range(Y):
            left_k(block).wait_send()

    @pl.when(owner)
    def _():
        for block in range(Z):
            for j in range(K):
                c = block * K + j

                @pl.when(jnp.logical_or(c != col, y != z))
                def _():
                    remote(EY, EX.at[x % 2, c], ez_s.at[0], ez_r.at[c], z=z).wait_recv()

            for t in (2, 1, 3):
                ex(block, t).start()

    for i in (7, 8, 9):
        fetch(i).wait()
    for t in range(Z):
        h_arrived(t * K + 1 - k)
    zeros = jnp.zeros((64, 256), BF16)
    for side in range(2):
        pay = jnp.concatenate(
            [pay_ref[...], zeros] if side == 0 else [zeros, pay_ref[...]], axis=0
        )
        for s in range(4):
            rows = HB[:, s * TOK : (s + 1) * TOK, :].reshape(NT, 128)
            VB[side * 4 + s] = dot(rows, pay).astype(BF16)
    GA[...] = jax.nn.sigmoid(dot(NB[...], sw_ref[...])).reshape(SEQ, 2, ROW, 256)

    head = iota((ROW, 256), 1) // 32
    for i in range(2):
        h = lax.rem(x + i, 2)

        @pl.when(x != 2 * k + h)
        def _():
            for block in range(Z):
                part = pl.ds(block * K, K)
                remote(
                    EX.at[h, part], EX.at[h, part], ex_s.at[0, 0], ex_r.at[h, block], x=x
                ).wait_recv()

        shifts = EX[h, :, TOK : TOK + 16, :].astype(F32)[:, 0:1, :]
        factor = jnp.exp(shifts - jnp.max(shifts, axis=0, keepdims=True))
        w = EX[h, :, 0:TOK, :].astype(F32) * factor
        total = jnp.sum(jnp.sum(w, axis=0, keepdims=True), axis=1, keepdims=True)
        weights = jnp.transpose((w / total).reshape(NT, 128)).astype(BF16)
        for s in range(SEQ):
            full = dot(weights, VB[s])
            average = jnp.zeros((ROW, 256), F32)
            for g in range(HEADS):
                average = jnp.where(head == g, full[g * ROW : (g + 1) * ROW], average)
            GB[s, h] = (GA[s, h] * average).astype(BF16)
    gated = GB[...].reshape(SEQ * TOK, 256)
    out = h_ref[...].reshape(SEQ * TOK, 64).astype(F32) + dot_nt(gated, rett_ref[...])
    align_ref[...] = out.astype(BF16).reshape(SEQ, TOK, 64)

    for block in range(Y):

        @pl.when(jnp.logical_not(e_here(block)))
        def _():
            ez(block).wait_send()

    @pl.when(owner)
    def _():
        for block in range(Z):
            for t in range(1, X):
                ex(block, t).wait_send()


def place_outputs(align_ref, pout_ref, align_out, pair_out, sems):
    copies = [
        pltpu.make_async_copy(pout_ref, pair_out, sems.at[0]),
        pltpu.make_async_copy(align_ref, align_out, sems.at[1]),
    ]
    for copy in copies:
        copy.start()
    for copy in copies:
        copy.wait()


def body(h, pair, seq, tok, pp, mm, sm, pay, sw, ret, ti, to, *, Y, Z):
    R, C = Y * X, Z * K
    NT = C * TOK
    dma = pltpu.SemaphoreType.DMA
    args = (h, pair, seq.reshape(1, -1), tok.reshape(1, -1), pp, mm)
    args += (sm.T, pay, sw, ret.T, ti, to)
    align, out = pl.pallas_call(
        functools.partial(kernel, Y, Z),
        out_shape=(
            pltpu.VMEM(h.shape, BF16),
            pltpu.VMEM(pair.shape, BF16),
        ),
        in_specs=[pl.BlockSpec(memory_space=pl.ANY)] * 12,
        out_specs=(pl.BlockSpec(memory_space=pltpu.VMEM),) * 2,
        scratch_shapes=[pltpu.VMEM(v.shape, v.dtype) for v in args]
        + [
            pltpu.VMEM((R, 16, 512), BF16),
            pltpu.VMEM((Z, 2, 16, 256), BF16),
            pltpu.VMEM((R, 16, 256), BF16),
            pltpu.VMEM((C, 128, 128), BF16),
            pltpu.VMEM((TOK + 16, 128), BF16),
            pltpu.VMEM((2, C, TOK + 16, 128), BF16),
            pltpu.VMEM((1024, 128), F32),
            pltpu.VMEM((4096, 512), BF16),
            pltpu.VMEM((128, 4096), BF16),
            pltpu.VMEM((1024, R * SEQ), BF16),
            pltpu.VMEM((SEQ, NT, 256), BF16),
            pltpu.VMEM((256, 64), BF16),
            pltpu.VMEM((512, 128), BF16),
            pltpu.VMEM((512, 128), BF16),
            pltpu.VMEM((SEQ, 2, ROW, 256), F32),
            pltpu.VMEM((SEQ, 2, ROW, 256), BF16),
            dma((12,)),
            dma((Y,)),
            dma((Y, X)),
            dma((R,)),
            dma((Z,)),
            dma((Z,)),
            dma((Z, 2)),
            dma((R,)),
            dma((Y,)),
            dma((Y,)),
            dma((Z,)),
            dma((Z,)),
            dma((C,)),
            dma((Y,)),
            dma((C,)),
            dma((Z, X)),
            dma((2, Z)),
        ],
        compiler_params=pltpu.CompilerParams(
            collective_id=0, has_side_effects=True, vmem_limit_bytes=60 * 1024 * 1024
        ),
        cost_estimate=pl.CostEstimate(
            flops=3_000_000_000, bytes_accessed=2_000_000, transcendentals=400_000
        ),
    )(*args)
    return pl.pallas_call(
        place_outputs,
        out_shape=(pltpu.HBM(h.shape, BF16), pltpu.HBM(pair.shape, BF16)),
        in_specs=[pl.BlockSpec(memory_space=pltpu.VMEM)] * 2,
        out_specs=(pl.BlockSpec(memory_space=pltpu.HBM),) * 2,
        scratch_shapes=[dma((2,))],
    )(
        pltpu.with_memory_space_constraint(align, pltpu.VMEM),
        pltpu.with_memory_space_constraint(out, pltpu.VMEM),
    )


def solution(mesh):
    Y, Z = mesh.shape["row"] // X, mesh.shape["col"] // K
    split = Mesh(mesh.devices.reshape(Y, X, Z, K), ("y", "x", "z", "k"))
    tiled = P(("y", "x"), ("z", "k"), None)
    return jax.shard_map(
        functools.partial(body, Y=Y, Z=Z),
        mesh=split,
        in_specs=(tiled, tiled) + (P(),) * 10,
        out_specs=(tiled, tiled),
        check_vma=False,
    )
```

```python
import functools

import jax
import jax.numpy as jnp
from jax import lax
from jax.experimental import pallas as pl
from jax.experimental.pallas import tpu as pltpu
from jax.sharding import Mesh
from jax.sharding import PartitionSpec as P

F32 = jnp.float32
BF16 = jnp.bfloat16
MESH = pl.DeviceIdType.MESH
epsilon = 1e-05

X, K = 4, 2
SEQ = 8
TOK = 32
ROW = 16
HEADS = 8


def iota(shape, dim):
    return lax.broadcasted_iota(jnp.int32, shape, dim)


def one_hot(condition):
    return jnp.where(condition, 1.0, 0.0).astype(BF16)


def dot(a, b):
    return jnp.dot(a, b, preferred_element_type=F32)


def dot_nt(a, b, precision=None):
    return lax.dot_general(
        a, b, (((1,), (1,)), ((), ())), precision=precision, preferred_element_type=F32
    )


def normalized(source):
    center = source - jnp.mean(source, axis=-1, keepdims=True)
    spread = jnp.mean(center * center, axis=-1, keepdims=True)
    return center * lax.rsqrt(spread + epsilon)


def kernel(Y, Z, *refs):
    R = Y * X
    C = Z * K
    NS = R * SEQ
    NT = C * TOK
    hbm, (align_ref, pout_ref), refs = refs[:12], refs[12:14], refs[14:]
    local, refs = refs[:12], refs[12:]
    h_ref, pair_ref, seq_ref, tok_ref, pp_ref, mm_ref = local[:6]
    smt_ref, pay_ref, sw_ref, rett_ref, ti_ref, to_ref = local[6:]
    RB, LZ, LB, HB, EY, EX, MF, WB, AB, RT, VB, NB, MID, PNB, GA, GB = refs[:16]
    in_s, ry_s, rx_s, r_r, lz_s, lz_r, lx_s, l_r, lk_s, lk_r = refs[16:26]
    hz_s, hk_s, h_r, ez_s, ez_r, ex_s, ex_r = refs[26:]
    y, x = lax.axis_index("y"), lax.axis_index("x")
    z, k = lax.axis_index("z"), lax.axis_index("k")
    row = y * X + x
    col = z * K + k
    owner = k == x // 2
    far_first = sorted(range(1, Z), key=lambda t: -min(t, Z - t))
    near_first = far_first[::-1]

    def remote(src, dst, send, recv, **to):
        return pltpu.make_async_remote_copy(
            src_ref=src,
            dst_ref=dst,
            send_sem=send,
            recv_sem=recv,
            device_id=to,
            device_id_type=MESH,
        )

    def fetch(i):
        return pltpu.make_async_copy(hbm[i], local[i], in_s.at[i])

    for i in (0, 4, 3, 2):
        fetch(i).start()

    barrier = pltpu.get_barrier_semaphore()
    steps = [(axis, t) for axis, n in (("y", Y), ("z", Z), ("x", X), ("k", K)) for t in range(1, n)]
    size, place = {"y": Y, "z": Z, "x": X, "k": K}, {"y": y, "z": z, "x": x, "k": k}
    for axis, t in sorted(steps, key=lambda step: -min(step[1], size[step[0]] - step[1])):
        pl.semaphore_signal(
            barrier,
            inc=1,
            device_id={axis: lax.rem(place[axis] + t, size[axis])},
            device_id_type=MESH,
        )

    for i in (5, 1, 6, 10, 11, 7, 8, 9):
        fetch(i).start()
    for i in (0, 4, 3, 2):
        fetch(i).wait()

    hf = h_ref[...].reshape(SEQ * TOK, 64).astype(F32)
    norm_f = normalized(hf)
    NB[...] = norm_f.astype(BF16)
    tokens = tok_ref[...].astype(F32)
    seqs = seq_ref[...].astype(F32)
    hit = iota((TOK, NT), 1) == col * TOK + iota((TOK, NT), 0)
    live_tok = jnp.sum(jnp.where(hit, tokens, 0.0), axis=1, keepdims=True)
    live_tok = jnp.concatenate([live_tok] * SEQ, axis=0)
    hit = iota((SEQ * TOK, NS), 1) == row * SEQ + iota((SEQ * TOK, NS), 0) // TOK
    live_seq = jnp.sum(jnp.where(hit, seqs, 0.0), axis=1, keepdims=True)
    inverse_count = 1.0 / jnp.maximum(jnp.sum(seqs, axis=1, keepdims=True), 1.0)
    norm = (norm_f * live_tok).astype(BF16)

    pp = pp_ref[...]
    mine = iota((256, 128), 0) % 4 == iota((256, 128), 1) // 32
    a, b = iota((64, 256), 0), iota((64, 256), 1)
    left_w = dot(pp, one_hot(iota((64, 128), 0) == iota((64, 128), 1) % 32)).astype(BF16)
    spread = dot(norm, left_w) * live_seq
    spread = jnp.where(mine, spread, 0.0).astype(BF16)
    pick = one_hot(
        (a % 8 == b // 32) & ((b % 32) // 4 == 4 * (a // 32) + 2 * ((a // 8) % 2) + (a // 16) % 2)
    )
    packed = dot(pick, spread).astype(BF16)
    for h in range(2):
        for t in range(2):
            LZ[z, h, :, t * 128 : (t + 1) * 128] = packed[(h * 2 + t) * 16 : (h * 2 + t + 1) * 16]

    right_t = dot_nt(one_hot(iota((32, 64), 1) == 32 + iota((32, 64), 0)), pp).astype(BF16)
    spread = []
    for s in range(SEQ):
        one = norm[s * TOK : (s + 1) * TOK]
        spread.append(dot_nt(right_t, jnp.concatenate([one] * 4, axis=0)))
    spread = jnp.concatenate(spread, axis=0)
    spread = jnp.where(mine, spread, 0.0).astype(BF16)
    pick = one_hot((a % 8 == b // 32) & ((b % 32) // 4 == ((a // 8) % 2) * 4 + a // 16))
    packed = dot(pick, spread).astype(BF16)
    for t in range(4):
        RB[row, :, t * 128 : (t + 1) * 128] = packed[t * 16 : (t + 1) * 16]

    pl.semaphore_wait(barrier, (Y - 1) + (Z - 1) + (X - 1) + (K - 1))

    def left_z(t):
        return remote(LZ.at[z], LZ.at[z], lz_s.at[t], lz_r.at[z], z=lax.rem(z + t, Z))

    def left_x(block, h):
        return remote(
            LZ.at[block, h],
            LB.at[row],
            lx_s.at[block, h],
            l_r.at[row],
            y=block,
            x=2 * k + h,
        )

    def left_here(block, h):
        return jnp.logical_and(block == y, 2 * k + h == x)

    def left_forward(block):
        for h in range(2):

            @pl.when(jnp.logical_not(left_here(block, h)))
            def _():
                left_x(block, h).start()

            @pl.when(left_here(block, h))
            def _():
                LB[row] = LZ[block, h]

    def left_k(block):
        part = pl.ds(block * X, X)
        return remote(LB.at[part], LB.at[part], lk_s.at[block], lk_r.at[block], k=1 - k)

    def right_y(t):
        return remote(RB.at[row], RB.at[row], ry_s.at[t], r_r.at[row], y=lax.rem(y + t, Y))

    def right_x(block, t):
        r = block * X + x
        return remote(
            RB.at[r], RB.at[r], rx_s.at[block, t], r_r.at[r], x=lax.rem(x + t, X)
        )

    def right_arrived(r):
        remote(RB.at[r], RB.at[r], ry_s.at[0], r_r.at[r], x=x).wait_recv()

    for t in far_first:
        left_z(t).start()
        right_y(t).start()
    for t in (2, 1, 3):
        right_x(y, t).start()

    u, v = iota((64, 128), 0), iota((64, 128), 1)
    HB[col] = (
        dot(norm[:128], one_hot(u == v)) + dot(norm[128:], one_hot(u + 64 == v))
    ).astype(BF16)

    fetch(5).wait()
    MF[...] = mm_ref[...].astype(F32)
    WB[...] = jnp.zeros_like(WB)
    for d in range(32):
        part = MF[pl.ds(d, 32, stride=32), :].astype(BF16)
        for i in range(4):
            WB[d * 128 + i * 32 : d * 128 + (i + 1) * 32, i * 128 : (i + 1) * 128] = part

    half = Y // 2
    outer = jnp.logical_or(z < Y // 4, z >= Y - Y // 4)

    def right_forward(block):
        @pl.when(block != y)
        def _():
            right_arrived(block * X + x)
            for t in (2, 1, 3):
                right_x(block, t).start()

    def left_next(block):
        @pl.when(block != z)
        def _():
            remote(
                LZ.at[block], LZ.at[block], lz_s.at[0], lz_r.at[block], z=z
            ).wait_recv()

        left_forward(block)

    for i in range(half):
        right_forward(i)
    for i in range(half):
        left_next(jnp.where(outer, i, half - 1 - i))
    def hz(t):
        return remote(HB.at[col], HB.at[col], hz_s.at[t], h_r.at[col], z=lax.rem(z + t, Z))

    def hk(block):
        c = block * K + k
        return remote(HB.at[c], HB.at[c], hk_s.at[block], h_r.at[c], k=1 - k)

    def h_arrived(c):
        remote(HB.at[c], HB.at[c], hz_s.at[0], h_r.at[c], z=z).wait_recv()

    for i in range(half, Y):
        block = jnp.where(outer, Y + half - 1 - i, i)
        right_forward(block)
        left_next(block)

    for t in far_first:
        hz(t).start()

    @pl.when(owner)
    def _():
        for block in range(Y):
            for other in range(X):
                r = block * X + other

                @pl.when(r != row)
                def _():
                    remote(LB.at[r], LB.at[r], lx_s.at[0, 0], l_r.at[r], x=x).wait_recv()

            left_k(block).start()

    for block in range(Y):
        for t in range(1, X):
            right_arrived(block * X + lax.rem(x + t, X))
    for half in range(2):
        right = RB[...].astype(F32).reshape(R, 2, SEQ, 512)[:, half].reshape(NS, 512)
        RT[half * 512 : (half + 1) * 512, :] = jnp.transpose(right).astype(BF16)

    @pl.when(jnp.logical_not(owner))
    def _():
        for block in range(Y):
            part = pl.ds(block * X, X)
            remote(LB.at[part], LB.at[part], lk_s.at[0], lk_r.at[block], y=y).wait_recv()

    left = LB[...].astype(F32).reshape(R, 2, SEQ, 256)
    left = jnp.concatenate(
        [left[:, 0].reshape(NS, 256), left[:, 1].reshape(NS, 256)], axis=1
    ).astype(BF16)
    for part in range(4):
        outer = dot(RT[part * 256 : (part + 1) * 256, :], left).astype(BF16)
        for dd in range(8):
            d = part * 8 + dd
            for g in range(4):
                AB[g * 32 : (g + 1) * 32, d * 128 : (d + 1) * 128] = outer[
                    dd * 32 : (dd + 1) * 32, g * 128 : (g + 1) * 128
                ]
    mean = dot(AB[...], WB[...]) * inverse_count
    mean = jnp.concatenate(
        [
            mean[(i // 4) * 32 : (i // 4 + 1) * 32, (i % 4) * 128 : (i % 4 + 1) * 128]
            for i in range(ROW)
        ],
        axis=0,
    )
    fetch(1).wait()
    fetch(6).wait()
    pair_mid = (pair_ref[...].reshape(ROW * TOK, 128).astype(F32) + mean).astype(BF16)
    MID[...] = pair_mid
    pair_norm = normalized(pair_mid.astype(F32))
    PNB[...] = pair_norm.astype(BF16)
    score_w = jnp.concatenate(
        [jnp.broadcast_to(smt_ref[h : h + 1, :], (ROW, 128)) for h in range(HEADS)], axis=0
    )
    every = dot_nt(pair_norm, score_w, lax.Precision.HIGHEST)
    lane_i = iota((TOK, 128), 1) % ROW
    scores = jnp.zeros((TOK, 128), F32)
    for i in range(ROW):
        scores = jnp.where(lane_i == i, every[i * TOK : (i + 1) * TOK], scores)
    shift = jnp.max(scores, axis=0, keepdims=True).astype(BF16).astype(F32)
    EY[0:TOK, :] = jnp.exp(scores - shift).astype(BF16)
    EY[TOK : TOK + 16, :] = jnp.broadcast_to(shift, (16, 128)).astype(BF16)

    def ez(to):
        return remote(
            EY, EX.at[x % 2, col], ez_s.at[to], ez_r.at[col], y=to, z=y, k=x // 2
        )

    def e_here(to):
        return jnp.logical_and(jnp.logical_and(to == y, z == y), owner)

    def ex(block, t):
        part = pl.ds(block * K, K)
        return remote(
            EX.at[x % 2, part],
            EX.at[x % 2, part],
            ex_s.at[block, t],
            ex_r.at[x % 2, block],
            x=lax.rem(x + t, X),
        )

    for to in range(Y):

        @pl.when(jnp.logical_not(e_here(to)))
        def _():
            ez(to).start()

        @pl.when(e_here(to))
        def _():
            EX[x % 2, col] = EY[...]

    hk(z).start()
    for t in near_first:
        block = lax.rem(z + t, Z)
        h_arrived(block * K + k)
        hk(block).start()
    fetch(10).wait()
    fetch(11).wait()
    for part in range(4):
        rows = slice(part * 128, (part + 1) * 128)
        pre = dot(PNB[rows, :], ti_ref[...])
        gate = pre[:, :512]
        hidden = (gate / (1.0 + jnp.exp(-gate)) * pre[:, 512:]).astype(BF16)
        out = (MID[rows, :].astype(F32) + dot(hidden, to_ref[...])).astype(BF16)
        pout_ref[part * 4 : (part + 1) * 4] = out.reshape(4, TOK, 128)

    for t in range(1, Y):
        right_y(t).wait_send()
    for block in range(Y):
        for t in range(1, X):
            right_x(block, t).wait_send()
    for t in range(1, Z):
        left_z(t).wait_send()
        hz(t).wait_send()
    for block in range(Z):
        hk(block).wait_send()
        for h in range(2):

            @pl.when(jnp.logical_not(left_here(block, h)))
            def _():
                left_x(block, h).wait_send()

    @pl.when(owner)
    def _():
        for block in range(Y):
            left_k(block).wait_send()

    @pl.when(owner)
    def _():
        for block in range(Z):
            for j in range(K):
                c = block * K + j

                @pl.when(jnp.logical_or(c != col, y != z))
                def _():
                    remote(EY, EX.at[x % 2, c], ez_s.at[0], ez_r.at[c], z=z).wait_recv()

            for t in (2, 1, 3):
                ex(block, t).start()

    for i in (7, 8, 9):
        fetch(i).wait()
    for t in range(Z):
        h_arrived(t * K + 1 - k)
    zeros = jnp.zeros((64, 256), BF16)
    for side in range(2):
        pay = jnp.concatenate(
            [pay_ref[...], zeros] if side == 0 else [zeros, pay_ref[...]], axis=0
        )
        for s in range(4):
            rows = HB[:, s * TOK : (s + 1) * TOK, :].reshape(NT, 128)
            VB[side * 4 + s] = dot(rows, pay).astype(BF16)
    GA[...] = jax.nn.sigmoid(dot(NB[...], sw_ref[...])).reshape(SEQ, 2, ROW, 256)

    head = iota((ROW, 256), 1) // 32
    for i in range(2):
        h = lax.rem(x + i, 2)

        @pl.when(x != 2 * k + h)
        def _():
            for block in range(Z):
                part = pl.ds(block * K, K)
                remote(
                    EX.at[h, part], EX.at[h, part], ex_s.at[0, 0], ex_r.at[h, block], x=x
                ).wait_recv()

        shifts = EX[h, :, TOK : TOK + 16, :].astype(F32)[:, 0:1, :]
        factor = jnp.exp(shifts - jnp.max(shifts, axis=0, keepdims=True))
        w = EX[h, :, 0:TOK, :].astype(F32) * factor
        total = jnp.sum(jnp.sum(w, axis=0, keepdims=True), axis=1, keepdims=True)
        weights = jnp.transpose((w / total).reshape(NT, 128)).astype(BF16)
        for s in range(SEQ):
            full = dot(weights, VB[s])
            average = jnp.zeros((ROW, 256), F32)
            for g in range(HEADS):
                average = jnp.where(head == g, full[g * ROW : (g + 1) * ROW], average)
            GB[s, h] = (GA[s, h] * average).astype(BF16)
    gated = GB[...].reshape(SEQ * TOK, 256)
    out = h_ref[...].reshape(SEQ * TOK, 64).astype(F32) + dot_nt(gated, rett_ref[...])
    align_ref[...] = out.astype(BF16).reshape(SEQ, TOK, 64)

    for block in range(Y):

        @pl.when(jnp.logical_not(e_here(block)))
        def _():
            ez(block).wait_send()

    @pl.when(owner)
    def _():
        for block in range(Z):
            for t in range(1, X):
                ex(block, t).wait_send()


def place_outputs(align_ref, pout_ref, align_out, pair_out, sems):
    copies = [
        pltpu.make_async_copy(pout_ref, pair_out, sems.at[0]),
        pltpu.make_async_copy(align_ref, align_out, sems.at[1]),
    ]
    for copy in copies:
        copy.start()
    for copy in copies:
        copy.wait()


def body(h, pair, seq, tok, pp, mm, sm, pay, sw, ret, ti, to, *, Y, Z):
    R, C = Y * X, Z * K
    NT = C * TOK
    dma = pltpu.SemaphoreType.DMA
    args = (h, pair, seq.reshape(1, -1), tok.reshape(1, -1), pp, mm)
    args += (sm.T, pay, sw, ret.T, ti, to)
    align, out = pl.pallas_call(
        functools.partial(kernel, Y, Z),
        out_shape=(
            pltpu.VMEM(h.shape, BF16),
            pltpu.VMEM(pair.shape, BF16),
        ),
        in_specs=[pl.BlockSpec(memory_space=pl.ANY)] * 12,
        out_specs=(pl.BlockSpec(memory_space=pltpu.VMEM),) * 2,
        scratch_shapes=[pltpu.VMEM(v.shape, v.dtype) for v in args]
        + [
            pltpu.VMEM((R, 16, 512), BF16),
            pltpu.VMEM((Z, 2, 16, 256), BF16),
            pltpu.VMEM((R, 16, 256), BF16),
            pltpu.VMEM((C, 128, 128), BF16),
            pltpu.VMEM((TOK + 16, 128), BF16),
            pltpu.VMEM((2, C, TOK + 16, 128), BF16),
            pltpu.VMEM((1024, 128), F32),
            pltpu.VMEM((4096, 512), BF16),
            pltpu.VMEM((128, 4096), BF16),
            pltpu.VMEM((1024, R * SEQ), BF16),
            pltpu.VMEM((SEQ, NT, 256), BF16),
            pltpu.VMEM((256, 64), BF16),
            pltpu.VMEM((512, 128), BF16),
            pltpu.VMEM((512, 128), BF16),
            pltpu.VMEM((SEQ, 2, ROW, 256), F32),
            pltpu.VMEM((SEQ, 2, ROW, 256), BF16),
            dma((12,)),
            dma((Y,)),
            dma((Y, X)),
            dma((R,)),
            dma((Z,)),
            dma((Z,)),
            dma((Z, 2)),
            dma((R,)),
            dma((Y,)),
            dma((Y,)),
            dma((Z,)),
            dma((Z,)),
            dma((C,)),
            dma((Y,)),
            dma((C,)),
            dma((Z, X)),
            dma((2, Z)),
        ],
        compiler_params=pltpu.CompilerParams(
            collective_id=0, has_side_effects=True, vmem_limit_bytes=60 * 1024 * 1024
        ),
        cost_estimate=pl.CostEstimate(
            flops=3_000_000_000, bytes_accessed=2_000_000, transcendentals=400_000
        ),
    )(*args)
    return pl.pallas_call(
        place_outputs,
        out_shape=(pltpu.HBM(h.shape, BF16), pltpu.HBM(pair.shape, BF16)),
        in_specs=[pl.BlockSpec(memory_space=pltpu.VMEM)] * 2,
        out_specs=(pl.BlockSpec(memory_space=pltpu.HBM),) * 2,
        scratch_shapes=[dma((2,))],
    )(
        pltpu.with_memory_space_constraint(align, pltpu.VMEM),
        pltpu.with_memory_space_constraint(out, pltpu.VMEM),
    )


def solution(mesh):
    Y, Z = mesh.shape["row"] // X, mesh.shape["col"] // K
    split = Mesh(mesh.devices.reshape(Y, X, Z, K), ("y", "x", "z", "k"))
    tiled = P(("y", "x"), ("z", "k"), None)
    return jax.shard_map(
        functools.partial(body, Y=Y, Z=Z),
        mesh=split,
        in_specs=(tiled, tiled) + (P(),) * 10,
        out_specs=(tiled, tiled),
        check_vma=False,
    )
```
